32 devices in a mesh: hst: 16 (over z, y, core), local: 2 (over x).
Axes of the slice: x: 2, y: 2, z: 4, core: 2. Of those that a mesh axis runs over, the one named last changes fastest.
Arguments:
- gate_act: bfloat16 [2048, 11008], P('hst', 'local'), may hold values from -6 to 6
- up_act: bfloat16 [2048, 11008], P('hst', 'local'), may hold values from -6 to 6
- cotangent: bfloat16 [2048, 4096], P('hst', 'local'), may hold values from -6 to 6
- down_weight: bfloat16 [11008, 4096], P('local', 'hst'), may hold values from -0.0546875 to 0.0546875
Outputs:
- output: bfloat16 [2048, 4096], P('hst', 'local')
- gate_delta: bfloat16 [2048, 11008], P('hst', 'local')
- up_delta: bfloat16 [2048, 11008], P('hst', 'local')
- down_grad: float32 [11008, 4096], P('local', 'hst')
The draws below stay inside these ranges and needn't reach their ends.
All inputs are finite; a program needn't handle non-finite values.
Results may differ from the reference program's by a relative error of at most 0.005.
Values may be sent and summed in bfloat16 or wider, within the bound.
No kernel may reach another device: no remote copies, remote signals or barrier semaphores. Data moves between devices by JAX's collectives and lax.ppermute only.
A program may use at most 320 MiB of HBM per device.

```python
import jax
import jax.numpy as jnp

D = 4096
FF = 11008
TOKENS = 2048


def raised(array, own_key, source, target, blocks, factor):
    def block_of(dim):
        return (jnp.arange(array.shape[dim]) // (array.shape[dim] // blocks)).reshape((-1,) + (1,) * (array.ndim - 1 - dim))

    one_side = jax.random.permutation(own_key, blocks)[block_of(target)]
    second = (block_of(target) + blocks // 2) % blocks
    return jnp.where((block_of(source) == one_side) | (block_of(source) == second), factor * array, array)


def level_of(key, extent, cuts, low, largest):
    loudness, own = 1.0, jax.random.fold_in(key, 6)
    for position, blocks in cuts:
        steps = jnp.exp(jax.random.uniform(jax.random.fold_in(own, position), (blocks,), jnp.float32, low / len(cuts), largest / len(cuts)))
        loudness = loudness * jnp.repeat(steps, extent[position] // blocks).reshape([-1 if axis == position else 1 for axis in range(len(extent))])
    return loudness


def bell_draw(stream_key, dims, spread, reach, cuts=(), dtype=jnp.bfloat16):
    entries = spread * jax.random.normal(stream_key, dims, jnp.float32)
    if cuts:
        entries = entries * level_of(stream_key, dims, cuts, -0.22, 0.18)
    return jnp.clip(entries, -reach, reach).astype(dtype)


def bell_draw_with(rng, extent, scale, most, cuts, heavy, dtype=jnp.bfloat16):
    result = scale * jax.random.normal(rng, extent, jnp.float32)
    if cuts:
        result = result * level_of(rng, extent, cuts, -0.22, 0.18)
    return jnp.clip(raised(result, jax.random.fold_in(rng, 3), *heavy), -most, most).astype(dtype)


def setup_inputs(seed: int = 0) -> dict:
    key_list = jax.random.split(jax.random.key(seed), 5)
    gate_act = bell_draw(key_list[0], (TOKENS, FF), 1.0, 6.0, ((0, 16), (1, 2)))
    up_act = bell_draw(key_list[1], (TOKENS, FF), 1.0, 6.0, ((0, 16), (1, 2)))
    cotangent = bell_draw_with(key_list[2], (TOKENS, D), 1.0, 6.0, ((0, 16), (1, 2)), (0, 1, 16, 2.0))
    down_weight = bell_draw(key_list[3], (FF, D), FF ** -0.5, 0.0546875, ((0, 2), (1, 16)))
    return {"gate_act": gate_act, "up_act": up_act, "cotangent": cotangent, "down_weight": down_weight}


def reference(gate_act, up_act, cotangent, down_weight):
    gate_wide = gate_act.astype(jnp.float32)
    up_wide = up_act.astype(jnp.float32)
    sigmoid_gate = jax.nn.sigmoid(gate_wide)
    hidden = (gate_wide * sigmoid_gate * up_wide).astype(jnp.bfloat16)
    output = jnp.dot(hidden, down_weight, preferred_element_type=jnp.float32).astype(jnp.bfloat16)
    hidden_grad = jnp.dot(cotangent, down_weight.T, preferred_element_type=jnp.float32)
    up_delta = (hidden_grad * gate_wide * sigmoid_gate).astype(jnp.bfloat16)
    gate_delta = (hidden_grad * up_wide * sigmoid_gate * (1.0 + gate_wide * (1.0 - sigmoid_gate))).astype(jnp.bfloat16)
    down_grad = jnp.dot(hidden.T, cotangent, preferred_element_type=jnp.float32)
    return output, gate_delta, up_delta, down_grad
```

```python
import jax
import jax.numpy as jnp
from jax import lax
from jax.sharding import PartitionSpec as P

QUAD = 4
CHUNKS = 2


def cuts(extent, parts):
    lanes = -(-extent // 128)
    edges = [min(extent, 128 * ((lanes * i + parts - 1) // parts)) for i in range(parts + 1)]
    return [(lo, hi) for lo, hi in zip(edges, edges[1:]) if hi > lo]


def solution(mesh):
    n_hst, n_local = mesh.shape["hst"], mesh.shape["local"]
    n_far = n_hst // QUAD

    def swap(value, bit):
        return lax.ppermute(value, "hst", [(h, h ^ bit) for h in range(n_hst)])

    def shift(value, step):
        pairs = [(h, (h + step * QUAD) % n_hst) for h in range(n_hst)]
        return lax.ppermute(value, "hst", pairs)

    def hop(value, way, sources):
        pairs = [(s * QUAD + q, (s + way) * QUAD + q) for s in sources for q in range(QUAD)]
        return lax.ppermute(value, "hst", pairs)

    def local_shift(value, step):
        return lax.ppermute(value, "local", [(i, (i + step) % n_local) for i in range(n_local)])

    def gather_far(own, far):
        above, below = {}, {}
        up = down = own
        for d in range(1, n_far):
            up = below[d] = hop(up, 1, range(d - 1, n_far - 1))
            down = above[d] = hop(down, -1, range(1, n_far - d + 1))
        slots = [own]
        for e in range(1, n_far):
            slots.append(jnp.where(far + e < n_far, above[e], below[n_far - e]))
        return jnp.concatenate(slots, axis=0)

    def reduce_far(slots):
        up = down = None
        for d in range(n_far - 1, 0, -1):
            up_term, down_term = slots[d], slots[n_far - d]
            if up is not None:
                up_term = up_term + up.astype(jnp.float32)
                down_term = down_term + down.astype(jnp.float32)
            up = hop(up_term.astype(jnp.bfloat16), 1, range(0, n_far - d))
            down = hop(down_term.astype(jnp.bfloat16), -1, range(d, n_far))
        return slots[0] + up.astype(jnp.float32) + down.astype(jnp.float32)

    def on_device(gate_act, up_act, cotangent, down_weight):
        h = lax.axis_index("hst")
        x = lax.axis_index("local")
        far, near = h // QUAD, h % QUAD
        tokens, half = cotangent.shape
        width = down_weight.shape[1]
        hidden_units = gate_act.shape[1]
        order = (0, 2, 1, 3)
        bounds = cuts(hidden_units, CHUNKS)

        parts = [cotangent]
        for step in range(1, n_local):
            parts.append(local_shift(cotangent, n_local - step))
        twice = jnp.concatenate(parts + parts[:-1], axis=1)
        cot_full = lax.dynamic_slice_in_dim(
            twice, ((n_local - x) % n_local) * half, n_local * half, axis=1
        )
        cot_view = cot_full.reshape(tokens, n_far, QUAD, width)
        cot_view = jnp.concatenate(
            [lax.dynamic_slice_in_dim(cot_view, near ^ k, 1, axis=2) for k in order], axis=2
        )
        cot_view = cot_view.reshape(tokens, n_far, QUAD * width)

        def cot_for(step):
            return lax.dynamic_index_in_dim(cot_view, (far + step) % n_far, axis=1, keepdims=False)

        cot_rows = jnp.concatenate(
            [cot_for(0)] + [shift(cot_for(n_far - e), n_far - e) for e in range(1, n_far)], axis=0
        )

        out_sum = 0.0
        gate_parts, up_parts, grad_parts = [], [], []
        for lo, hi in bounds:
            gate_wide = gate_act[:, lo:hi].astype(jnp.float32)
            up_wide = up_act[:, lo:hi].astype(jnp.float32)
            sigmoid_gate = jax.nn.sigmoid(gate_wide)
            hidden = (gate_wide * sigmoid_gate * up_wide).astype(jnp.bfloat16)

            weight = down_weight[lo:hi]
            pair = jnp.concatenate([weight, swap(weight, 2)], axis=1)
            weight_cols = jnp.concatenate([pair, swap(pair, 1)], axis=1)

            terms = lax.dot_general(
                cot_rows, weight_cols, (((1,), (1,)), ((), ())), preferred_element_type=jnp.float32
            )
            hidden_grad = reduce_far([terms[e * tokens : (e + 1) * tokens] for e in range(n_far)])
            up_parts.append((hidden_grad * gate_wide * sigmoid_gate).astype(jnp.bfloat16))
            gate_parts.append(
                (
                    hidden_grad * up_wide * sigmoid_gate * (1.0 + gate_wide * (1.0 - sigmoid_gate))
                ).astype(jnp.bfloat16)
            )

            hidden_rows = gather_far(hidden, far)
            out_sum = out_sum + jnp.dot(
                hidden_rows, weight_cols, preferred_element_type=jnp.float32
            )
            grad = lax.dot_general(
                hidden_rows, cot_rows, (((0,), (0,)), ((), ())), preferred_element_type=jnp.float32
            )
            theirs = swap(grad[:, 2 * width :].astype(jnp.bfloat16), 1)
            grad = grad[:, : 2 * width] + theirs.astype(jnp.float32)
            theirs = swap(grad[:, width:].astype(jnp.bfloat16), 2)
            grad_parts.append(grad[:, :width] + theirs.astype(jnp.float32))

        out_terms = out_sum.astype(jnp.bfloat16)
        slots = [out_terms[:tokens]]
        for e in range(1, n_far):
            slots.append(shift(out_terms[e * tokens : (e + 1) * tokens], e))
        back = [slots[0]] + slots[:0:-1]
        twice = jnp.concatenate(back + back[:-1], axis=1)
        columns = QUAD * width
        mine = lax.dynamic_slice_in_dim(
            twice, ((n_far - far) % n_far) * columns, n_far * columns, axis=1
        )
        mine = mine.reshape(tokens, n_far, QUAD, width)
        mine = jnp.concatenate(
            [lax.dynamic_slice_in_dim(mine, slot, 1, axis=2) for slot in slot_of(near)],
            axis=2,
        )
        mine = mine.reshape(tokens, n_local, half)

        def half_of(step):
            return lax.dynamic_index_in_dim(mine, (x + step) % n_local, axis=1, keepdims=False)

        output = half_of(0).astype(jnp.float32)
        for step in range(1, n_local):
            output = output + local_shift(half_of(step), step).astype(jnp.float32)
        return (
            output.astype(jnp.bfloat16),
            jnp.concatenate(gate_parts, axis=1),
            jnp.concatenate(up_parts, axis=1),
            jnp.concatenate(grad_parts, axis=0),
        )

    def slot_of(near):
        result = []
        for block in range(QUAD):
            k = near ^ block
            result.append(((k & 1) << 1) | (k >> 1))
        return result

    specs = (P("hst", "local"), P("hst", "local"), P("hst", "local"), P("local", "hst"))
    return jax.shard_map(
        on_device, mesh=mesh, in_specs=specs, out_specs=specs, check_vma=False
    )
```

```python
import jax
import jax.numpy as jnp
from jax import lax
from jax.sharding import PartitionSpec as P

QUAD = 4
CHUNKS = 2


def cuts(extent, parts):
    lanes = -(-extent // 128)
    edges = [min(extent, 128 * ((lanes * i + parts - 1) // parts)) for i in range(parts + 1)]
    return [(lo, hi) for lo, hi in zip(edges, edges[1:]) if hi > lo]


def solution(mesh):
    n_hst, n_local = mesh.shape["hst"], mesh.shape["local"]
    n_far = n_hst // QUAD

    def swap(value, bit):
        return lax.ppermute(value, "hst", [(h, h ^ bit) for h in range(n_hst)])

    def shift(value, step):
        pairs = [(h, (h + step * QUAD) % n_hst) for h in range(n_hst)]
        return lax.ppermute(value, "hst", pairs)

    def hop(value, way, sources):
        pairs = [(s * QUAD + q, (s + way) * QUAD + q) for s in sources for q in range(QUAD)]
        return lax.ppermute(value, "hst", pairs)

    def local_shift(value, step):
        return lax.ppermute(value, "local", [(i, (i + step) % n_local) for i in range(n_local)])

    far_groups = [[f * QUAD + q for f in range(n_far)] for q in range(QUAD)]

    def gather_far(own, far):
        return lax.all_gather(own, "hst", axis=0, tiled=True, axis_index_groups=far_groups)

    def reduce_far(slots):
        up = down = None
        for d in range(n_far - 1, 0, -1):
            up_term, down_term = slots[d], slots[n_far - d]
            if up is not None:
                up_term = up_term + up.astype(jnp.float32)
                down_term = down_term + down.astype(jnp.float32)
            up = hop(up_term.astype(jnp.bfloat16), 1, range(0, n_far - d))
            down = hop(down_term.astype(jnp.bfloat16), -1, range(d, n_far))
        return slots[0] + up.astype(jnp.float32) + down.astype(jnp.float32)

    def on_device(gate_act, up_act, cotangent, down_weight):
        h = lax.axis_index("hst")
        x = lax.axis_index("local")
        far, near = h // QUAD, h % QUAD
        tokens, half = cotangent.shape
        width = down_weight.shape[1]
        hidden_units = gate_act.shape[1]
        order = (0, 2, 1, 3)
        bounds = cuts(hidden_units, CHUNKS)

        parts = [cotangent]
        for step in range(1, n_local):
            parts.append(local_shift(cotangent, n_local - step))
        twice = jnp.concatenate(parts + parts[:-1], axis=1)
        cot_full = lax.dynamic_slice_in_dim(
            twice, ((n_local - x) % n_local) * half, n_local * half, axis=1
        )
        cot_view = cot_full.reshape(tokens, n_far, QUAD, width)
        cot_view = jnp.concatenate(
            [lax.dynamic_slice_in_dim(cot_view, near ^ k, 1, axis=2) for k in order], axis=2
        )
        cot_view = cot_view.reshape(tokens, n_far, QUAD * width)

        def cot_for(step):
            return lax.dynamic_index_in_dim(cot_view, (far + step) % n_far, axis=1, keepdims=False)

        cot_rows = jnp.concatenate(
            [cot_for(0)] + [shift(cot_for(n_far - e), n_far - e) for e in range(1, n_far)], axis=0
        )

        twice = jnp.concatenate([cot_rows, cot_rows[:-tokens]], axis=0)
        cot_sorted = lax.dynamic_slice_in_dim(
            twice, ((n_far - far) % n_far) * tokens, n_far * tokens, axis=0
        )

        out_sum = 0.0
        gate_parts, up_parts, grad_parts = [], [], []
        for lo, hi in bounds:
            gate_wide = gate_act[:, lo:hi].astype(jnp.float32)
            up_wide = up_act[:, lo:hi].astype(jnp.float32)
            sigmoid_gate = jax.nn.sigmoid(gate_wide)
            hidden = (gate_wide * sigmoid_gate * up_wide).astype(jnp.bfloat16)

            weight = down_weight[lo:hi]
            pair = jnp.concatenate([weight, swap(weight, 2)], axis=1)
            weight_cols = jnp.concatenate([pair, swap(pair, 1)], axis=1)

            terms = lax.dot_general(
                cot_rows, weight_cols, (((1,), (1,)), ((), ())), preferred_element_type=jnp.float32
            )
            hidden_grad = reduce_far([terms[e * tokens : (e + 1) * tokens] for e in range(n_far)])
            up_parts.append((hidden_grad * gate_wide * sigmoid_gate).astype(jnp.bfloat16))
            gate_parts.append(
                (
                    hidden_grad * up_wide * sigmoid_gate * (1.0 + gate_wide * (1.0 - sigmoid_gate))
                ).astype(jnp.bfloat16)
            )

            hidden_rows = gather_far(hidden, far)
            out_sum = out_sum + jnp.dot(
                hidden_rows, weight_cols, preferred_element_type=jnp.float32
            )
            grad = lax.dot_general(
                hidden_rows, cot_sorted, (((0,), (0,)), ((), ())), preferred_element_type=jnp.float32
            )
            theirs = swap(grad[:, 2 * width :].astype(jnp.bfloat16), 1)
            grad = grad[:, : 2 * width] + theirs.astype(jnp.float32)
            theirs = swap(grad[:, width:].astype(jnp.bfloat16), 2)
            grad_parts.append(grad[:, :width] + theirs.astype(jnp.float32))

        out_terms = out_sum.astype(jnp.bfloat16)

        def out_for(step):
            return lax.dynamic_slice_in_dim(
                out_terms, ((far + step) % n_far) * tokens, tokens, axis=0
            )

        slots = [out_for(0)]
        for e in range(1, n_far):
            slots.append(shift(out_for(e), e))
        back = [slots[0]] + slots[:0:-1]
        twice = jnp.concatenate(back + back[:-1], axis=1)
        columns = QUAD * width
        mine = lax.dynamic_slice_in_dim(
            twice, ((n_far - far) % n_far) * columns, n_far * columns, axis=1
        )
        mine = mine.reshape(tokens, n_far, QUAD, width)
        mine = jnp.concatenate(
            [lax.dynamic_slice_in_dim(mine, slot, 1, axis=2) for slot in slot_of(near)],
            axis=2,
        )
        mine = mine.reshape(tokens, n_local, half)

        def half_of(step):
            return lax.dynamic_index_in_dim(mine, (x + step) % n_local, axis=1, keepdims=False)

        output = half_of(0).astype(jnp.float32)
        for step in range(1, n_local):
            output = output + local_shift(half_of(step), step).astype(jnp.float32)
        return (
            output.astype(jnp.bfloat16),
            jnp.concatenate(gate_parts, axis=1),
            jnp.concatenate(up_parts, axis=1),
            jnp.concatenate(grad_parts, axis=0),
        )

    def slot_of(near):
        result = []
        for block in range(QUAD):
            k = near ^ block
            result.append(((k & 1) << 1) | (k >> 1))
        return result

    specs = (P("hst", "local"), P("hst", "local"), P("hst", "local"), P("local", "hst"))
    return jax.shard_map(
        on_device, mesh=mesh, in_specs=specs, out_specs=specs, check_vma=False
    )
```

```python
import jax
import jax.numpy as jnp
from jax import lax
from jax.sharding import PartitionSpec as P

QUAD = 4
STREAMS = 2
PER_STREAM = 2
ORDER = (0, 2, 1, 3)


def after(value, *others):
    return lax.optimization_barrier((value,) + others)[0]


def slot_of(near):
    result = []
    for block in range(QUAD):
        k = near ^ block
        result.append(((k & 1) << 1) | (k >> 1))
    return result


def solution(mesh):
    n_hst, n_local = mesh.shape["hst"], mesh.shape["local"]
    n_far = n_hst // QUAD

    def swap(value, bit):
        return lax.ppermute(value, "hst", [(h, h ^ bit) for h in range(n_hst)])

    def shift(value, step):
        pairs = [(h, (h + step * QUAD) % n_hst) for h in range(n_hst)]
        return lax.ppermute(value, "hst", pairs)

    def hop(value, way, sources):
        pairs = [(s * QUAD + q, (s + way) * QUAD + q) for s in sources for q in range(QUAD)]
        return lax.ppermute(value, "hst", pairs)

    def local_shift(value, step):
        return lax.ppermute(value, "local", [(i, (i + step) % n_local) for i in range(n_local)])

    def on_device(gate_act, up_act, cotangent, down_weight):
        h = lax.axis_index("hst")
        x = lax.axis_index("local")
        far, near = h // QUAD, h % QUAD
        tokens, half = cotangent.shape
        width = down_weight.shape[1]
        hidden_units = gate_act.shape[1]
        n_chunks = STREAMS * PER_STREAM
        lanes = -(-hidden_units // 128)
        chunk = 128 * -(-lanes // n_chunks)
        bounds = [(f * chunk, min(hidden_units, (f + 1) * chunk)) for f in range(n_chunks)]

        def padded(value, axis):
            missing = [(0, 0), (0, 0)]
            missing[axis] = (0, chunk - value.shape[axis])
            return jnp.pad(value, missing) if missing[axis][1] else value

        parts = [cotangent]
        for step in range(1, n_local):
            parts.append(local_shift(cotangent, n_local - step))
        twice = jnp.concatenate(parts + parts[:-1], axis=1)
        cot_full = lax.dynamic_slice_in_dim(
            twice, ((n_local - x) % n_local) * half, n_local * half, axis=1
        )
        cot_view = cot_full.reshape(tokens, n_far, QUAD, width)
        cot_view = jnp.concatenate(
            [lax.dynamic_slice_in_dim(cot_view, near ^ k, 1, axis=2) for k in ORDER], axis=2
        )
        cot_view = cot_view.reshape(tokens, n_far, QUAD * width)

        def cot_for(step):
            return lax.dynamic_index_in_dim(cot_view, (far + step) % n_far, axis=1, keepdims=False)

        cot_rows = jnp.concatenate(
            [cot_for(0)] + [shift(cot_for(n_far - e), n_far - e) for e in range(1, n_far)], axis=0
        )

        weights, last = [], []
        for f, (lo, hi) in enumerate(bounds):
            weight = after(padded(down_weight[lo:hi], 0), *last)
            other = swap(weight, 2)
            last = [other]
            if f == 0:
                last.append(parts[1])
            if f == 1:
                last.append(cot_rows)
            pair = jnp.concatenate([weight, other], axis=1)
            weights.append(jnp.concatenate([pair, swap(pair, 1)], axis=1))

        wide, hidden, terms = {}, {}, {}
        for f, (lo, hi) in enumerate(bounds):
            gate_wide = padded(gate_act[:, lo:hi], 1).astype(jnp.float32)
            up_wide = padded(up_act[:, lo:hi], 1).astype(jnp.float32)
            sigmoid_gate = jax.nn.sigmoid(gate_wide)
            wide[f] = gate_wide, up_wide, sigmoid_gate
            hidden[f] = (gate_wide * sigmoid_gate * up_wide).astype(jnp.bfloat16)

        gate_parts, up_parts, grad_parts, out_sums = {}, {}, {}, {}
        ready = []

        def gathered(f, above, below):
            slots = [hidden[f]]
            for e in range(1, n_far):
                slots.append(jnp.where(far + e < n_far, above[e], below[n_far - e]))
            hidden_rows = jnp.concatenate(slots, axis=0)
            out_sums[f] = jnp.dot(hidden_rows, weights[f], preferred_element_type=jnp.float32)
            grad = lax.dot_general(
                hidden_rows, cot_rows, (((0,), (0,)), ((), ())), preferred_element_type=jnp.float32
            )
            theirs = swap(grad[:, 2 * width :].astype(jnp.bfloat16), 1)
            grad = grad[:, : 2 * width] + theirs.astype(jnp.float32)
            theirs = swap(after(grad[:, width:].astype(jnp.bfloat16), *last), 2)
            last[:] = [theirs]
            ready.append(theirs)
            lo, hi = bounds[f]
            grad_parts[f] = (grad[:, :width] + theirs.astype(jnp.float32))[: hi - lo]

        def reduced(f, hidden_grad):
            gate_wide, up_wide, sigmoid_gate = wide[f]
            keep = bounds[f][1] - bounds[f][0]
            up_parts[f] = (hidden_grad * gate_wide * sigmoid_gate).astype(jnp.bfloat16)[:, :keep]
            gate_parts[f] = (
                hidden_grad * up_wide * sigmoid_gate * (1.0 + gate_wide * (1.0 - sigmoid_gate))
            ).astype(jnp.bfloat16)[:, :keep]

        def stream(chunks):
            recv = None
            for step in range(len(chunks) + 1):
                gather = chunks[step] if step < len(chunks) else None
                reduce = chunks[step - 1] if step else None
                if reduce is not None:
                    dots = lax.dot_general(
                        cot_rows,
                        weights[reduce],
                        (((1,), (1,)), ((), ())),
                        preferred_element_type=jnp.float32,
                    )
                    slots = [dots[e * tokens : (e + 1) * tokens] for e in range(n_far)]
                above, below = {}, {}
                first = 1 if gather is not None else 2
                end = n_far if reduce is not None else n_far - 1
                for j in range(first, end + 1):
                    lowest = 0 if reduce is not None and j > 1 else j - 1
                    highest = n_far - 2 if gather is not None and j < n_far else j - 2
                    sending = []
                    for which, place in ((0, far), (1, n_far - 1 - far)):
                        if j == 1:
                            if recv is None:
                                sending.append(hidden[gather])
                            else:
                                sending.append(after(hidden[gather], recv[which]))
                            continue
                        summed = None
                        if reduce is not None:
                            d = n_far - j + 1
                            summed = slots[d if which == 0 else n_far - d]
                            if j > 2:
                                summed = summed + recv[which].astype(jnp.float32)
                            summed = summed.astype(jnp.bfloat16)
                        if gather is None or j == n_far:
                            sending.append(summed)
                        elif reduce is None:
                            sending.append(recv[which])
                        else:
                            sending.append(jnp.where(place >= j - 1, recv[which], summed))
                    recv = yield sending, range(lowest, highest + 1)
                    if gather is not None and j < n_far:
                        below[j], above[j] = recv
                    if gather is not None and j == n_far - 1:
                        gathered(gather, above, below)
                if reduce is not None:
                    total = slots[0] + recv[0].astype(jnp.float32) + recv[1].astype(jnp.float32)
                    reduced(reduce, total)

        streams = [stream(range(s, n_chunks, STREAMS)) for s in range(STREAMS)]
        total_slots = STREAMS * (PER_STREAM + 1) * n_far - 2 * STREAMS
        recvs, history = [None] * STREAMS, []
        alive = list(range(STREAMS))
        awaited = 0
        while alive:
            for s in list(alive):
                try:
                    (up, down), sources = streams[s].send(recvs[s])
                except StopIteration:
                    alive.remove(s)
                    continue
                slot = len(history)
                others = history[-STREAMS - 1] if slot > STREAMS else ()
                if awaited < len(ready) and 10 * slot >= total_slots * (6 + awaited):
                    others += (ready[awaited],)
                    awaited += 1
                if others:
                    up, down = lax.optimization_barrier((up, down) + others)[:2]
                downs = [n_far - 1 - z for z in sources]
                recvs[s] = hop(up, 1, sources), hop(down, -1, downs)
                history.append(recvs[s])

        out_terms = sum(out_sums[f] for f in range(n_chunks)).astype(jnp.bfloat16)
        slots = [out_terms[:tokens]]
        for e in range(1, n_far):
            slots.append(shift(out_terms[e * tokens : (e + 1) * tokens], e))
        back = [slots[0]] + slots[:0:-1]
        twice = jnp.concatenate(back + back[:-1], axis=1)
        columns = QUAD * width
        mine = lax.dynamic_slice_in_dim(
            twice, ((n_far - far) % n_far) * columns, n_far * columns, axis=1
        )
        mine = mine.reshape(tokens, n_far, QUAD, width)
        mine = jnp.concatenate(
            [lax.dynamic_slice_in_dim(mine, slot, 1, axis=2) for slot in slot_of(near)], axis=2
        )
        mine = mine.reshape(tokens, n_local, half)

        def half_of(step):
            return lax.dynamic_index_in_dim(mine, (x + step) % n_local, axis=1, keepdims=False)

        output = half_of(0).astype(jnp.float32)
        for step in range(1, n_local):
            output = output + local_shift(half_of(step), step).astype(jnp.float32)
        chunks = range(n_chunks)
        return (
            output.astype(jnp.bfloat16),
            jnp.concatenate([gate_parts[f] for f in chunks], axis=1),
            jnp.concatenate([up_parts[f] for f in chunks], axis=1),
            jnp.concatenate([grad_parts[f] for f in chunks], axis=0),
        )

    specs = (P("hst", "local"), P("hst", "local"), P("hst", "local"), P("local", "hst"))
    return jax.shard_map(
        on_device, mesh=mesh, in_specs=specs, out_specs=specs, check_vma=False
    )
```

```python
import jax
import jax.numpy as jnp
from jax import lax
from jax.sharding import PartitionSpec as P

QUAD = 4
CHUNKS = 2
ORDER = (0, 2, 1, 3)


def after(value, *others):
    return lax.optimization_barrier((value,) + others)[0]


def slot_of(near):
    result = []
    for block in range(QUAD):
        k = near ^ block
        result.append(((k & 1) << 1) | (k >> 1))
    return result


def solution(mesh):
    n_hst, n_local = mesh.shape["hst"], mesh.shape["local"]
    n_far = n_hst // QUAD

    def swap(value, bit):
        return lax.ppermute(value, "hst", [(h, h ^ bit) for h in range(n_hst)])

    def shift(value, step):
        pairs = [(h, (h + step * QUAD) % n_hst) for h in range(n_hst)]
        return lax.ppermute(value, "hst", pairs)

    def hop(value, way, sources):
        pairs = [(s * QUAD + q, (s + way) * QUAD + q) for s in sources for q in range(QUAD)]
        return lax.ppermute(value, "hst", pairs)

    def local_shift(value, step):
        return lax.ppermute(value, "local", [(i, (i + step) % n_local) for i in range(n_local)])

    def on_device(gate_act, up_act, cotangent, down_weight):
        h = lax.axis_index("hst")
        x = lax.axis_index("local")
        far, near = h // QUAD, h % QUAD
        tokens, half = cotangent.shape
        width = down_weight.shape[1]
        hidden_units = gate_act.shape[1]
        n_chunks = CHUNKS
        lanes = -(-hidden_units // 128)
        chunk = 128 * -(-lanes // n_chunks)
        bounds = [(f * chunk, min(hidden_units, (f + 1) * chunk)) for f in range(n_chunks)]

        parts = [cotangent]
        for step in range(1, n_local):
            parts.append(local_shift(cotangent, n_local - step))
        twice = jnp.concatenate(parts + parts[:-1], axis=1)
        cot_full = lax.dynamic_slice_in_dim(
            twice, ((n_local - x) % n_local) * half, n_local * half, axis=1
        )
        cot_view = cot_full.reshape(tokens, n_far, QUAD, width)
        cot_view = jnp.concatenate(
            [lax.dynamic_slice_in_dim(cot_view, near ^ k, 1, axis=2) for k in ORDER], axis=2
        )
        cot_view = cot_view.reshape(tokens, n_far, QUAD * width)

        def cot_for(step):
            return lax.dynamic_index_in_dim(cot_view, (far + step) % n_far, axis=1, keepdims=False)

        cot_rows = jnp.concatenate(
            [cot_for(0)] + [shift(cot_for(n_far - e), n_far - e) for e in range(1, n_far)], axis=0
        )

        weights, last = [], []
        for f, (lo, hi) in enumerate(bounds):
            weight = after(down_weight[lo:hi], *last)
            other = swap(weight, 2)
            last = [other]
            if f == 0:
                last.append(parts[1])
            if f == 1:
                last.append(cot_rows)
            pair = jnp.concatenate([weight, other], axis=1)
            weights.append(jnp.concatenate([pair, swap(pair, 1)], axis=1))

        wide, hidden, terms = {}, {}, {}
        for f, (lo, hi) in enumerate(bounds):
            gate_wide = gate_act[:, lo:hi].astype(jnp.float32)
            up_wide = up_act[:, lo:hi].astype(jnp.float32)
            sigmoid_gate = jax.nn.sigmoid(gate_wide)
            wide[f] = gate_wide, up_wide, sigmoid_gate
            hidden[f] = (gate_wide * sigmoid_gate * up_wide).astype(jnp.bfloat16)

        gate_parts, up_parts, grad_parts, out_sums = {}, {}, {}, {}
        ready = []

        def gathered(f, above, below):
            slots = [hidden[f]]
            for e in range(1, n_far):
                slots.append(jnp.where(far + e < n_far, above[e], below[n_far - e]))
            hidden_rows = jnp.concatenate(slots, axis=0)
            out_sums[f] = jnp.dot(hidden_rows, weights[f], preferred_element_type=jnp.float32)
            grad = lax.dot_general(
                hidden_rows, cot_rows, (((0,), (0,)), ((), ())), preferred_element_type=jnp.float32
            )
            theirs = swap(grad[:, 2 * width :].astype(jnp.bfloat16), 1)
            ready.append(theirs)
            grad = grad[:, : 2 * width] + theirs.astype(jnp.float32)
            theirs = swap(after(grad[:, width:].astype(jnp.bfloat16), *last), 2)
            last[:] = [theirs]
            grad_parts[f] = grad[:, :width] + theirs.astype(jnp.float32)

        def reduced(f, hidden_grad):
            gate_wide, up_wide, sigmoid_gate = wide[f]
            up_parts[f] = (hidden_grad * gate_wide * sigmoid_gate).astype(jnp.bfloat16)
            gate_parts[f] = (
                hidden_grad * up_wide * sigmoid_gate * (1.0 + gate_wide * (1.0 - sigmoid_gate))
            ).astype(jnp.bfloat16)

        history = []

        def both_ways(up, down, sources, *awaited):
            if len(history) > 2:
                awaited += history[-3]
            if awaited:
                up, down = lax.optimization_barrier((up, down) + awaited)[:2]
            downs = [n_far - 1 - z for z in sources]
            history.append((hop(up, 1, sources), hop(down, -1, downs)))
            return history[-1]

        def gather_rounds(f):
            above, below = {}, {}
            up = down = hidden[f]
            for j in range(1, n_far):
                up, down = both_ways(
                    up, down, range(j - 1, n_far - 1), *([cot_rows] if j == n_far - 1 else [])
                )
                below[j], above[j] = up, down
                if j == n_far - 1:
                    gathered(f, above, below)
                yield

        def reduce_rounds(f):
            terms = lax.dot_general(
                cot_rows, weights[f], (((1,), (1,)), ((), ())), preferred_element_type=jnp.float32
            )
            slots = [terms[e * tokens : (e + 1) * tokens] for e in range(n_far)]
            up = down = None
            for d in range(n_far - 1, 0, -1):
                up_term, down_term = slots[d], slots[n_far - d]
                if up is not None:
                    up_term = up_term + up.astype(jnp.float32)
                    down_term = down_term + down.astype(jnp.float32)
                up, down = both_ways(
                    up_term.astype(jnp.bfloat16),
                    down_term.astype(jnp.bfloat16),
                    range(0, n_far - d),
                    *(ready[f : f + 1] if d == 1 else []),
                )
                if d == 1:
                    reduced(f, slots[0] + up.astype(jnp.float32) + down.astype(jnp.float32))
                yield

        gathers = [gather_rounds(f) for f in range(n_chunks)]
        reduces = [reduce_rounds(f) for f in range(n_chunks)]
        gather_order = [gathers[f] for j in range(1, n_far) for f in range(n_chunks)]
        reduce_order = [reduces[f] for j in range(1, n_far) for f in range(n_chunks)]
        lag = len(gather_order) - n_chunks + 1
        order = gather_order[:lag]
        for i, rounds in enumerate(reduce_order):
            order += [rounds] + gather_order[lag + i : lag + i + 1]
        for rounds in order:
            next(rounds)

        out_terms = sum(out_sums[f] for f in range(n_chunks)).astype(jnp.bfloat16)
        slots = [out_terms[:tokens]]
        for e in range(1, n_far):
            slots.append(shift(out_terms[e * tokens : (e + 1) * tokens], e))
        back = [slots[0]] + slots[:0:-1]
        twice = jnp.concatenate(back + back[:-1], axis=1)
        columns = QUAD * width
        mine = lax.dynamic_slice_in_dim(
            twice, ((n_far - far) % n_far) * columns, n_far * columns, axis=1
        )
        mine = mine.reshape(tokens, n_far, QUAD, width)
        mine = jnp.concatenate(
            [lax.dynamic_slice_in_dim(mine, slot, 1, axis=2) for slot in slot_of(near)], axis=2
        )
        mine = mine.reshape(tokens, n_local, half)

        def half_of(step):
            return lax.dynamic_index_in_dim(mine, (x + step) % n_local, axis=1, keepdims=False)

        output = half_of(0).astype(jnp.float32)
        for step in range(1, n_local):
            output = output + local_shift(half_of(step), step).astype(jnp.float32)
        chunks = range(n_chunks)
        return (
            output.astype(jnp.bfloat16),
            jnp.concatenate([gate_parts[f] for f in chunks], axis=1),
            jnp.concatenate([up_parts[f] for f in chunks], axis=1),
            jnp.concatenate([grad_parts[f] for f in chunks], axis=0),
        )

    specs = (P("hst", "local"), P("hst", "local"), P("hst", "local"), P("local", "hst"))
    return jax.shard_map(
        on_device, mesh=mesh, in_specs=specs, out_specs=specs, check_vma=False
    )
```

```python
import jax
import jax.numpy as jnp
from jax import lax
from jax.sharding import PartitionSpec as P

QUAD = 4
CHUNKS = 2
ORDER = (0, 2, 1, 3)


def after(value, *others):
    return lax.optimization_barrier((value,) + others)[0]


def slot_of(near):
    result = []
    for block in range(QUAD):
        k = near ^ block
        result.append(((k & 1) << 1) | (k >> 1))
    return result


def solution(mesh):
    n_hst, n_local = mesh.shape["hst"], mesh.shape["local"]
    n_far = n_hst // QUAD

    def swap(value, bit):
        return lax.ppermute(value, "hst", [(h, h ^ bit) for h in range(n_hst)])

    def shift(value, step):
        pairs = [(h, (h + step * QUAD) % n_hst) for h in range(n_hst)]
        return lax.ppermute(value, "hst", pairs)

    def hop(value, way, sources):
        pairs = [(s * QUAD + q, (s + way) * QUAD + q) for s in sources for q in range(QUAD)]
        return lax.ppermute(value, "hst", pairs)

    def local_shift(value, step):
        return lax.ppermute(value, "local", [(i, (i + step) % n_local) for i in range(n_local)])

    def on_device(gate_act, up_act, cotangent, down_weight):
        h = lax.axis_index("hst")
        x = lax.axis_index("local")
        far, near = h // QUAD, h % QUAD
        tokens, half = cotangent.shape
        width = down_weight.shape[1]
        hidden_units = gate_act.shape[1]
        n_chunks = CHUNKS
        lanes = -(-hidden_units // 128)
        chunk = 128 * -(-lanes // n_chunks)
        bounds = [(f * chunk, min(hidden_units, (f + 1) * chunk)) for f in range(n_chunks)]

        cot_full = lax.all_gather(cotangent, "local", axis=1, tiled=True)
        cot_view = cot_full.reshape(tokens, n_far, QUAD, width)
        cot_view = jnp.concatenate(
            [lax.dynamic_slice_in_dim(cot_view, near ^ k, 1, axis=2) for k in ORDER], axis=2
        )
        cot_view = cot_view.reshape(tokens, n_far, QUAD * width)

        def cot_for(step):
            return lax.dynamic_index_in_dim(cot_view, (far + step) % n_far, axis=1, keepdims=False)

        cot_rows = jnp.concatenate(
            [cot_for(0)] + [shift(cot_for(n_far - e), n_far - e) for e in range(1, n_far)], axis=0
        )

        last, history = [], []
        got = {"x": cot_full, "cot": cot_rows}
        own_pairs, weights = [], {}
        for f, (lo, hi) in enumerate(bounds):
            weight = after(down_weight[lo:hi], *last)
            other = got["wy", f] = swap(weight, 2)
            last = [other, cot_full]
            own_pairs.append((weight, other))

        def weight_cols(f):
            if f not in weights:
                pair = jnp.concatenate(own_pairs[f], axis=1)
                far_pair = got["wc", f] = swap(after(pair, cot_full, *history[2 * f], *history[2 * f + 1]), 1)
                weights[f] = jnp.concatenate([pair, far_pair], axis=1)
            return weights[f]

        wide, hidden = {}, {}
        for f, (lo, hi) in enumerate(bounds):
            gate_wide = gate_act[:, lo:hi].astype(jnp.float32)
            up_wide = up_act[:, lo:hi].astype(jnp.float32)
            sigmoid_gate = jax.nn.sigmoid(gate_wide)
            wide[f] = gate_wide, up_wide, sigmoid_gate
            hidden[f] = (gate_wide * sigmoid_gate * up_wide).astype(jnp.bfloat16)

        hidden = lax.optimization_barrier(hidden)
        gate_parts, up_parts, grad_parts, out_sums = {}, {}, {}, {}

        def gathered(f, above, below):
            slots = [hidden[f]]
            for e in range(1, n_far):
                slots.append(jnp.where(far + e < n_far, above[e], below[n_far - e]))
            hidden_rows = jnp.concatenate(slots, axis=0)
            out_sums[f] = jnp.dot(hidden_rows, weight_cols(f), preferred_element_type=jnp.float32)
            grad = lax.dot_general(
                hidden_rows, cot_rows, (((0,), (0,)), ((), ())), preferred_element_type=jnp.float32
            )
            theirs = swap(grad[:, 2 * width :].astype(jnp.bfloat16), 1)
            got["gc", f] = theirs
            grad = grad[:, : 2 * width] + theirs.astype(jnp.float32)
            theirs = swap(after(grad[:, width:].astype(jnp.bfloat16), *last), 2)
            last[:] = [theirs]
            got["gy", f] = theirs
            grad_parts[f] = grad[:, :width] + theirs.astype(jnp.float32)

        def reduced(f, hidden_grad):
            gate_wide, up_wide, sigmoid_gate = wide[f]
            up_parts[f] = (hidden_grad * gate_wide * sigmoid_gate).astype(jnp.bfloat16)
            gate_parts[f] = (
                hidden_grad * up_wide * sigmoid_gate * (1.0 + gate_wide * (1.0 - sigmoid_gate))
            ).astype(jnp.bfloat16)

        rounds_in_all = 2 * (n_far - 1) * n_chunks
        due = [
            (2, "x"),
            (3, ("wy", 0)),
            (5, "cot"),
            (5, ("wc", 0)),
            (6, ("wy", 1)),
            (7, ("wc", 1)),
            (9, ("gc", 0)),
            (10, ("gc", 1)),
            (11, ("gy", 0)),
            (11, "out"),
        ]

        def both_ways(up, down, sources):
            now = len(history)
            awaited = history[-2] if now > 1 else ()
            for place, key in list(due):
                if key in got and now * 12 >= place * rounds_in_all:
                    awaited += tuple(got[key]) if key == "out" else (got[key],)
                    due.remove((place, key))
            if awaited:
                up, down = lax.optimization_barrier((up, down) + awaited)[:2]
            downs = [n_far - 1 - z for z in sources]
            history.append((hop(up, 1, sources), hop(down, -1, downs)))
            return history[-1]

        def gather_rounds(f):
            above, below = {}, {}
            up = down = hidden[f]
            for j in range(1, n_far):
                up, down = both_ways(up, down, range(j - 1, n_far - 1))
                below[j], above[j] = up, down
                if j == n_far - 1:
                    gathered(f, above, below)
                yield

        def reduce_rounds(f):
            terms = lax.dot_general(
                cot_rows, weight_cols(f), (((1,), (1,)), ((), ())), preferred_element_type=jnp.float32
            )
            slots = [terms[e * tokens : (e + 1) * tokens] for e in range(n_far)]
            up = down = None
            for d in range(n_far - 1, 0, -1):
                up_term, down_term = slots[d], slots[n_far - d]
                if up is not None:
                    up_term = up_term + up.astype(jnp.float32)
                    down_term = down_term + down.astype(jnp.float32)
                up, down = both_ways(
                    up_term.astype(jnp.bfloat16),
                    down_term.astype(jnp.bfloat16),
                    range(0, n_far - d),
                )
                if d == 1:
                    reduced(f, slots[0] + up.astype(jnp.float32) + down.astype(jnp.float32))
                yield

        def send_outputs():
            out_terms = sum(out_sums[f] for f in range(n_chunks)).astype(jnp.bfloat16)
            out_terms = after(out_terms, *history[9 * rounds_in_all // 12])
            slots = [out_terms[:tokens]]
            for e in range(1, n_far):
                slots.append(shift(out_terms[e * tokens : (e + 1) * tokens], e))
            return slots

        gathers = [gather_rounds(f) for f in range(n_chunks)]
        reduces = [reduce_rounds(f) for f in range(n_chunks)]
        gather_order = [gathers[f] for j in range(1, n_far) for f in range(n_chunks)]
        reduce_order = [
            reduces[f] for _, f in sorted((j + f, f) for j in range(1, n_far) for f in range(n_chunks))
        ]
        lag = len(gather_order) - n_chunks
        order = gather_order[:lag] + reduce_order[:1] + gather_order[lag:] + reduce_order[1:]
        for turn, rounds in enumerate(order):
            if turn == len(order) - 1:
                got["out"] = send_outputs()
            next(rounds)

        slots = got["out"]
        back = [slots[0]] + slots[:0:-1]
        twice = jnp.concatenate(back + back[:-1], axis=1)
        columns = QUAD * width
        mine = lax.dynamic_slice_in_dim(
            twice, ((n_far - far) % n_far) * columns, n_far * columns, axis=1
        )
        mine = mine.reshape(tokens, n_far, QUAD, width)
        mine = jnp.concatenate(
            [lax.dynamic_slice_in_dim(mine, slot, 1, axis=2) for slot in slot_of(near)], axis=2
        )
        mine = mine.reshape(tokens, n_local, half)

        def half_of(step):
            return lax.dynamic_index_in_dim(mine, (x + step) % n_local, axis=1, keepdims=False)

        output = half_of(0).astype(jnp.float32)
        for step in range(1, n_local):
            output = output + local_shift(half_of(step), step).astype(jnp.float32)
        chunks = range(n_chunks)
        return (
            output.astype(jnp.bfloat16),
            jnp.concatenate([gate_parts[f] for f in chunks], axis=1),
            jnp.concatenate([up_parts[f] for f in chunks], axis=1),
            jnp.concatenate([grad_parts[f] for f in chunks], axis=0),
        )

    specs = (P("hst", "local"), P("hst", "local"), P("hst", "local"), P("local", "hst"))
    return jax.shard_map(
        on_device, mesh=mesh, in_specs=specs, out_specs=specs, check_vma=False
    )
```

```python
import jax
import jax.numpy as jnp
from jax import lax
from jax.sharding import PartitionSpec as P

QUAD = 4
ORDER = (0, 2, 1, 3)


def after(value, *others):
    return lax.optimization_barrier((value,) + others)[0]


def slot_of(near):
    result = []
    for block in range(QUAD):
        k = near ^ block
        result.append(((k & 1) << 1) | (k >> 1))
    return result


def solution(mesh):
    n_hst, n_local = mesh.shape["hst"], mesh.shape["local"]
    n_far = n_hst // QUAD

    def swap(value, bit):
        return lax.ppermute(value, "hst", [(h, h ^ bit) for h in range(n_hst)])

    def shift(value, step):
        pairs = [(h, (h + step * QUAD) % n_hst) for h in range(n_hst)]
        return lax.ppermute(value, "hst", pairs)

    def hop(value, way, sources):
        pairs = [(s * QUAD + q, (s + way) * QUAD + q) for s in sources for q in range(QUAD)]
        return lax.ppermute(value, "hst", pairs)

    far_groups = [[f * QUAD + q for f in range(n_far)] for q in range(QUAD)]

    def local_shift(value, step):
        return lax.ppermute(value, "local", [(i, (i + step) % n_local) for i in range(n_local)])

    def on_device(gate_act, up_act, cotangent, down_weight):
        h = lax.axis_index("hst")
        x = lax.axis_index("local")
        far, near = h // QUAD, h % QUAD
        tokens, half = cotangent.shape
        width = down_weight.shape[1]
        hidden_units = gate_act.shape[1]
        n_chunks = 2
        first = 128 * (hidden_units * 24 // (43 * 128))
        bounds = [(0, first), (first, hidden_units)]

        parts = [cotangent]
        for step in range(1, n_local):
            parts.append(local_shift(cotangent, n_local - step))
        twice = jnp.concatenate(parts + parts[:-1], axis=1)
        cot_full = lax.dynamic_slice_in_dim(
            twice, ((n_local - x) % n_local) * half, n_local * half, axis=1
        )
        cot_view = cot_full.reshape(tokens, n_far, QUAD, width)
        cot_view = jnp.concatenate(
            [lax.dynamic_slice_in_dim(cot_view, near ^ k, 1, axis=2) for k in ORDER], axis=2
        )
        cot_view = cot_view.reshape(tokens, n_far, QUAD * width)

        def cot_for(step):
            return lax.dynamic_index_in_dim(cot_view, (far + step) % n_far, axis=1, keepdims=False)

        cot_rows = jnp.concatenate(
            [cot_for(0)] + [shift(cot_for(n_far - e), n_far - e) for e in range(1, n_far)], axis=0
        )

        twice = jnp.concatenate([cot_rows, cot_rows[:-tokens]], axis=0)
        cot_sorted = lax.dynamic_slice_in_dim(
            twice, ((n_far - far) % n_far) * tokens, n_far * tokens, axis=0
        )

        last, history = [parts[1]], []
        got, weights, own_pairs = {}, {}, []
        for f, (lo, hi) in enumerate(bounds):
            weight = after(down_weight[lo:hi], *last)
            other = swap(weight, 2)
            last = [other]
            own_pairs.append((weight, other))

        def weight_cols(f):
            if f not in weights:
                pair = jnp.concatenate(own_pairs[f], axis=1)
                far_pair = swap(after(pair, cot_rows, *(history[0] if f else ())), 1)
                weights[f] = jnp.concatenate([pair, far_pair], axis=1)
            return weights[f]

        wide, hidden = {}, {}
        for f, (lo, hi) in enumerate(bounds):
            gate_wide = gate_act[:, lo:hi].astype(jnp.float32)
            up_wide = up_act[:, lo:hi].astype(jnp.float32)
            sigmoid_gate = jax.nn.sigmoid(gate_wide)
            wide[f] = gate_wide, up_wide, sigmoid_gate
            hidden[f] = (gate_wide * sigmoid_gate * up_wide).astype(jnp.bfloat16)

        hidden = lax.optimization_barrier(hidden)
        gate_parts, up_parts, grad_parts, out_sums = {}, {}, {}, {}

        def gathered(f):
            hidden_rows = after(got["hidden", f], *history[-1])
            out_sums[f] = jnp.dot(hidden_rows, weight_cols(f), preferred_element_type=jnp.float32)
            grad = lax.dot_general(
                hidden_rows, cot_sorted, (((0,), (0,)), ((), ())), preferred_element_type=jnp.float32
            )
            theirs = swap(grad[:, 2 * width :].astype(jnp.bfloat16), 1)
            got["gc", f] = theirs
            grad = grad[:, : 2 * width] + theirs.astype(jnp.float32)
            theirs = swap(after(grad[:, width:].astype(jnp.bfloat16), *last), 2)
            last[:] = [theirs]
            got["gy", f] = theirs
            grad_parts[f] = grad[:, :width] + theirs.astype(jnp.float32)

        def reduced(f, hidden_grad):
            gate_wide, up_wide, sigmoid_gate = wide[f]
            up_parts[f] = (hidden_grad * gate_wide * sigmoid_gate).astype(jnp.bfloat16)
            gate_parts[f] = (
                hidden_grad * up_wide * sigmoid_gate * (1.0 + gate_wide * (1.0 - sigmoid_gate))
            ).astype(jnp.bfloat16)

        rounds_in_all = (n_far - 1) * n_chunks
        due = [(2, ("hidden", 0)), (3, ("gc", 0)), (5, ("gy", 0))]

        def both_ways(up, down, sources):
            now = len(history)
            awaited = history[-2] if now > 1 else ()
            for place, key in list(due):
                if key in got and now * 6 >= place * rounds_in_all:
                    awaited += (got[key],)
                    due.remove((place, key))
            if awaited:
                up, down = lax.optimization_barrier((up, down) + awaited)[:2]
            downs = [n_far - 1 - z for z in sources]
            history.append((hop(up, 1, sources), hop(down, -1, downs)))
            return history[-1]

        def reduce_rounds(f):
            terms = lax.dot_general(
                cot_rows, weight_cols(f), (((1,), (1,)), ((), ())), preferred_element_type=jnp.float32
            )
            slots = [terms[e * tokens : (e + 1) * tokens] for e in range(n_far)]
            up = down = None
            for d in range(n_far - 1, 0, -1):
                up_term, down_term = slots[d], slots[n_far - d]
                if up is not None:
                    up_term = up_term + up.astype(jnp.float32)
                    down_term = down_term + down.astype(jnp.float32)
                up, down = both_ways(
                    up_term.astype(jnp.bfloat16),
                    down_term.astype(jnp.bfloat16),
                    range(0, n_far - d),
                )
                if d == 1:
                    reduced(f, slots[0] + up.astype(jnp.float32) + down.astype(jnp.float32))
                yield

        for f in range(n_chunks):
            got["hidden", f] = lax.all_gather(
                after(hidden[f], parts[1]) if f else hidden[f],
                "hst",
                axis=0,
                tiled=True,
                axis_index_groups=far_groups,
            )
        reduces = [reduce_rounds(f) for f in range(n_chunks)]
        for j in range(1, n_far):
            for f, rounds in enumerate(reduces):
                next(rounds)
                if len(history) in (1, 4):
                    gathered(len(history) // 4)

        out_terms = sum(out_sums[f] for f in range(n_chunks)).astype(jnp.bfloat16)
        out_terms = after(out_terms, got["gc", n_chunks - 1])

        def out_for(step):
            return lax.dynamic_slice_in_dim(
                out_terms, ((far + step) % n_far) * tokens, tokens, axis=0
            )

        slots = [out_for(0)] + [shift(out_for(e), e) for e in range(1, n_far)]
        back = [slots[0]] + slots[:0:-1]
        twice = jnp.concatenate(back + back[:-1], axis=1)
        columns = QUAD * width
        mine = lax.dynamic_slice_in_dim(
            twice, ((n_far - far) % n_far) * columns, n_far * columns, axis=1
        )
        mine = mine.reshape(tokens, n_far, QUAD, width)
        mine = jnp.concatenate(
            [lax.dynamic_slice_in_dim(mine, slot, 1, axis=2) for slot in slot_of(near)], axis=2
        )
        mine = mine.reshape(tokens, n_local, half)

        def half_of(step):
            return lax.dynamic_index_in_dim(mine, (x + step) % n_local, axis=1, keepdims=False)

        output = half_of(0).astype(jnp.float32)
        for step in range(1, n_local):
            output = output + local_shift(half_of(step), step).astype(jnp.float32)
        chunks = range(n_chunks)
        return (
            output.astype(jnp.bfloat16),
            jnp.concatenate([gate_parts[f] for f in chunks], axis=1),
            jnp.concatenate([up_parts[f] for f in chunks], axis=1),
            jnp.concatenate([grad_parts[f] for f in chunks], axis=0),
        )

    specs = (P("hst", "local"), P("hst", "local"), P("hst", "local"), P("local", "hst"))
    return jax.shard_map(
        on_device, mesh=mesh, in_specs=specs, out_specs=specs, check_vma=False
    )
```

```python
import jax
import jax.numpy as jnp
from jax import lax
from jax.sharding import PartitionSpec as P

QUAD = 4
CHUNKS = 2
ORDER = (0, 2, 1, 3)


def after(value, *others):
    return lax.optimization_barrier((value,) + others)[0]


def slot_of(near):
    result = []
    for block in range(QUAD):
        k = near ^ block
        result.append(((k & 1) << 1) | (k >> 1))
    return result


def solution(mesh):
    n_hst, n_local = mesh.shape["hst"], mesh.shape["local"]
    n_far = n_hst // QUAD

    def swap(value, bit):
        return lax.ppermute(value, "hst", [(h, h ^ bit) for h in range(n_hst)])

    def shift(value, step):
        pairs = [(h, (h + step * QUAD) % n_hst) for h in range(n_hst)]
        return lax.ppermute(value, "hst", pairs)

    def hop(value, way, sources):
        pairs = [(s * QUAD + q, (s + way) * QUAD + q) for s in sources for q in range(QUAD)]
        return lax.ppermute(value, "hst", pairs)

    def local_shift(value, step):
        return lax.ppermute(value, "local", [(i, (i + step) % n_local) for i in range(n_local)])

    def on_device(gate_act, up_act, cotangent, down_weight):
        h = lax.axis_index("hst")
        x = lax.axis_index("local")
        far, near = h // QUAD, h % QUAD
        tokens, half = cotangent.shape
        width = down_weight.shape[1]
        hidden_units = gate_act.shape[1]
        n_chunks = CHUNKS
        lanes = -(-hidden_units // 128)
        chunk = 128 * -(-lanes // n_chunks)
        bounds = [(f * chunk, min(hidden_units, (f + 1) * chunk)) for f in range(n_chunks)]

        cot_full = lax.all_gather(cotangent, "local", axis=1, tiled=True)
        cot_view = cot_full.reshape(tokens, n_far, QUAD, width)
        cot_view = jnp.concatenate(
            [lax.dynamic_slice_in_dim(cot_view, near ^ k, 1, axis=2) for k in ORDER], axis=2
        )
        cot_view = cot_view.reshape(tokens, n_far, QUAD * width)

        def cot_for(step):
            return lax.dynamic_index_in_dim(cot_view, (far + step) % n_far, axis=1, keepdims=False)

        cot_rows = jnp.concatenate(
            [cot_for(0)] + [shift(cot_for(n_far - e), n_far - e) for e in range(1, n_far)], axis=0
        )

        last, history = [], []
        got = {"x": cot_full, "cot": cot_rows}
        own_pairs, weights = [], {}
        for f, (lo, hi) in enumerate(bounds):
            weight = after(down_weight[lo:hi], *last)
            other = swap(weight, 2)
            last = [other]
            own_pairs.append((weight, other))

        def weight_cols(f):
            if f not in weights:
                pair = jnp.concatenate(own_pairs[f], axis=1)
                far_pair = got["wc", f] = swap(after(pair, cot_full, *history[f]), 1)
                weights[f] = jnp.concatenate([pair, far_pair], axis=1)
            return weights[f]

        gate_all, up_all = gate_act.astype(jnp.float32), up_act.astype(jnp.float32)
        hidden = (gate_all * jax.nn.sigmoid(gate_all) * up_all).astype(jnp.bfloat16)
        gate_parts, up_parts, grad_parts = {}, {}, {}
        last_hop = n_far - 1

        def gathered(above, below):
            slots = [hidden]
            for e in range(1, n_far):
                slots.append(jnp.where(far + e < n_far, above[e], below[n_far - e]))
            rows = got["hidden"] = jnp.concatenate(slots, axis=0)
            for f, (lo, hi) in enumerate(bounds):
                grad = lax.dot_general(
                    rows[:, lo:hi],
                    cot_rows,
                    (((0,), (0,)), ((), ())),
                    preferred_element_type=jnp.float32,
                )
                theirs = grad[:, 2 * width :].astype(jnp.bfloat16)
                theirs = got["gc", f] = swap(after(theirs, got["gc", f - 1]) if f else theirs, 1)
                grad = grad[:, : 2 * width] + theirs.astype(jnp.float32)
                theirs = swap(after(grad[:, width:].astype(jnp.bfloat16), *last), 2)
                last[:] = [theirs]
                got["gy", f] = theirs
                grad_parts[f] = grad[:, :width] + theirs.astype(jnp.float32)

        def reduced(f, hidden_grad):
            lo, hi = bounds[f]
            gate_wide, up_wide = gate_act[:, lo:hi].astype(jnp.float32), up_act[:, lo:hi].astype(jnp.float32)
            sigmoid_gate = jax.nn.sigmoid(gate_wide)
            up_parts[f] = (hidden_grad * gate_wide * sigmoid_gate).astype(jnp.bfloat16)
            gate_parts[f] = (
                hidden_grad * up_wide * sigmoid_gate * (1.0 + gate_wide * (1.0 - sigmoid_gate))
            ).astype(jnp.bfloat16)

        awaited_by = {
            ("A", 2): ["x"],
            ("A", last_hop): ["cot", ("wc", 0)],
            ("R", 1, 1): [("gc", 0)],
            ("R", last_hop, 1): ["out"],
        }

        def both_ways(label, up, down, sources):
            awaited = history[-2] if len(history) > 1 else ()
            for key in awaited_by.get(label, ()):
                awaited += tuple(got[key]) if key == "out" else (got[key],)
            if awaited:
                up, down = lax.optimization_barrier((up, down) + awaited)[:2]
            downs = [n_far - 1 - z for z in sources]
            history.append((hop(up, 1, sources), hop(down, -1, downs)))
            return history[-1]

        def gather_rounds():
            above, below = {}, {}
            up = down = hidden
            for j in range(1, n_far):
                up, down = both_ways(("A", j), up, down, range(j - 1, n_far - 1))
                below[j], above[j] = up, down
                if j == last_hop:
                    gathered(above, below)
                yield

        def reduce_rounds(f):
            terms = lax.dot_general(
                cot_rows,
                weight_cols(f),
                (((1,), (1,)), ((), ())),
                preferred_element_type=jnp.float32,
            )
            slots = [terms[e * tokens : (e + 1) * tokens] for e in range(n_far)]
            up = down = None
            for j in range(1, n_far):
                d = n_far - j
                up_term, down_term = slots[d], slots[n_far - d]
                if up is not None:
                    up_term = up_term + up.astype(jnp.float32)
                    down_term = down_term + down.astype(jnp.float32)
                up, down = both_ways(
                    ("R", j, f),
                    up_term.astype(jnp.bfloat16),
                    down_term.astype(jnp.bfloat16),
                    range(0, n_far - d),
                )
                if j == last_hop:
                    reduced(f, slots[0] + up.astype(jnp.float32) + down.astype(jnp.float32))
                yield

        def send_outputs():
            out_sum = sum(
                jnp.dot(got["hidden"][:, lo:hi], weight_cols(f), preferred_element_type=jnp.float32)
                for f, (lo, hi) in enumerate(bounds)
            )
            out_terms = after(out_sum.astype(jnp.bfloat16), got["gc", n_chunks - 1])
            slots = [out_terms[:tokens]]
            for e in range(1, n_far):
                slots.append(shift(out_terms[e * tokens : (e + 1) * tokens], e))
            return slots

        gathers = gather_rounds()
        reduces = [reduce_rounds(f) for f in range(n_chunks)]
        turns = sorted((j + f, f) for j in range(1, n_far) for f in range(n_chunks))
        reduce_order = [reduces[f] for _, f in turns]
        order = [gathers] * (last_hop - 1) + reduce_order[:1] + [gathers] + reduce_order[1:]
        for turn, rounds in enumerate(order):
            if turn == len(order) - 1:
                got["out"] = send_outputs()
            next(rounds)

        slots = got["out"]
        back = [slots[0]] + slots[:0:-1]
        twice = jnp.concatenate(back + back[:-1], axis=1)
        columns = QUAD * width
        mine = lax.dynamic_slice_in_dim(
            twice, ((n_far - far) % n_far) * columns, n_far * columns, axis=1
        )
        mine = mine.reshape(tokens, n_far, QUAD, width)
        mine = jnp.concatenate(
            [lax.dynamic_slice_in_dim(mine, slot, 1, axis=2) for slot in slot_of(near)], axis=2
        )
        mine = mine.reshape(tokens, n_local, half)

        def half_of(step):
            return lax.dynamic_index_in_dim(mine, (x + step) % n_local, axis=1, keepdims=False)

        output = half_of(0).astype(jnp.float32)
        for step in range(1, n_local):
            output = output + local_shift(half_of(step), step).astype(jnp.float32)
        chunks = range(n_chunks)
        return (
            output.astype(jnp.bfloat16),
            jnp.concatenate([gate_parts[f] for f in chunks], axis=1),
            jnp.concatenate([up_parts[f] for f in chunks], axis=1),
            jnp.concatenate([grad_parts[f] for f in chunks], axis=0),
        )

    specs = (P("hst", "local"), P("hst", "local"), P("hst", "local"), P("local", "hst"))
    return jax.shard_map(
        on_device, mesh=mesh, in_specs=specs, out_specs=specs, check_vma=False
    )
```

```python
import jax
import jax.numpy as jnp
from jax import lax
from jax.sharding import PartitionSpec as P

QUAD = 4
ORDER = (0, 2, 1, 3)
KEEP_COLS = (((1,), (1,)), ((), ()))
SUM_ROWS = (((0,), (0,)), ((), ()))


def after(value, *others):
    return lax.optimization_barrier((value,) + others)[0] if others else value


def slot_of(near):
    return [((near ^ block) & 1) << 1 | (near ^ block) >> 1 for block in range(QUAD)]


def picked(view, places, axis):
    return jnp.concatenate(
        [lax.dynamic_slice_in_dim(view, place, 1, axis=axis) for place in places], axis=axis
    )


def solution(mesh):
    n_hst, n_local = mesh.shape["hst"], mesh.shape["local"]
    n_far = n_hst // QUAD
    last_hop = n_far - 1

    def swap(value, bit):
        return lax.ppermute(value, "hst", [(h, h ^ bit) for h in range(n_hst)])

    def shift(value, step):
        pairs = [(h, (h + step * QUAD) % n_hst) for h in range(n_hst)]
        return lax.ppermute(value, "hst", pairs)

    def hop(value, way, sources):
        pairs = [(s * QUAD + q, (s + way) * QUAD + q) for s in sources for q in range(QUAD)]
        return lax.ppermute(value, "hst", pairs)

    def both_ways(up, down, sources):
        return hop(up, 1, sources), hop(down, -1, [n_far - 1 - z for z in sources])

    def local_shift(value, step):
        return lax.ppermute(value, "local", [(i, (i + step) % n_local) for i in range(n_local)])

    def on_device(gate_act, up_act, cotangent, down_weight):
        h = lax.axis_index("hst")
        x = lax.axis_index("local")
        far, near = h // QUAD, h % QUAD
        tokens, half = cotangent.shape
        width = down_weight.shape[1]
        columns = QUAD * width
        hidden_units = gate_act.shape[1]
        per_half = half // columns
        middle = 128 * ((hidden_units // 128 + 1) // 2)
        bounds = [(0, middle), (middle, hidden_units)]

        fence = []

        def move(send, value, *args):
            return send(after(value, *fence), *args)

        hidden, wide = [], []
        for lo, hi in bounds:
            gate_wide = gate_act[:, lo:hi].astype(jnp.float32)
            up_wide = up_act[:, lo:hi].astype(jnp.float32)
            sigmoid_gate = jax.nn.sigmoid(gate_wide)
            wide.append((gate_wide, up_wide, sigmoid_gate))
            hidden.append((gate_wide * sigmoid_gate * up_wide).astype(jnp.bfloat16))

        above, below = ({}, {}), ({}, {})
        travel = {}

        def gather_hop(f, j):
            up, down = travel.get(("A", f), (hidden[f], hidden[f]))
            up, down = (after(up, *fence), after(down, *fence))
            up, down = travel["A", f] = both_ways(up, down, range(j - 1, n_far - 1))
            below[f][j], above[f][j] = up, down
            return [up, down]

        def reduce_hop(f, j):
            d = n_far - j
            up_term, down_term = terms[f][d], terms[f][n_far - d]
            if j > 1:
                up, down = travel["R", f]
                up_term = up_term + up.astype(jnp.float32)
                down_term = down_term + down.astype(jnp.float32)
            up, down = after(up_term.astype(jnp.bfloat16), *fence), after(
                down_term.astype(jnp.bfloat16), *fence
            )
            travel["R", f] = both_ways(up, down, range(0, j))
            return list(travel["R", f])

        def weight_columns(f, other):
            lo, hi = bounds[f]
            pair = jnp.concatenate([down_weight[lo:hi], other], axis=1)
            return jnp.concatenate([pair, move(swap, pair, 1)], axis=1)

        def reduce_terms(f):
            dots = lax.dot_general(
                cot_rows, weights[f], KEEP_COLS, preferred_element_type=jnp.float32
            )
            return [dots[e * tokens : (e + 1) * tokens] for e in range(n_far)]

        def gathered_rows(f):
            slots = [hidden[f]]
            for e in range(1, n_far):
                slots.append(jnp.where(far + e < n_far, above[f][e], below[f][n_far - e]))
            return jnp.concatenate(slots, axis=0)

        def grad_terms(f):
            keep, give = (
                lax.dot_general(rows[f], part, SUM_ROWS, preferred_element_type=jnp.float32)
                for part in (cot_rows[:, : 2 * width], cot_rows[:, 2 * width :])
            )
            theirs = move(swap, give.astype(jnp.bfloat16), 1).astype(jnp.float32)
            return (
                keep[:, :width] + theirs[:, :width],
                (keep[:, width:] + theirs[:, width:]).astype(jnp.bfloat16),
            )

        weights, terms, rows, out_sums, grads = {}, {}, {}, {}, {}

        own_cot = picked(
            cotangent.reshape(tokens, per_half, QUAD, width), [near ^ k for k in ORDER], 2
        ).reshape(tokens, half)
        parts = [own_cot] + [local_shift(own_cot, n_local - s) for s in range(1, n_local)]
        weight_side = swap(down_weight[:middle], 2)
        fence = gather_hop(0, 1) + parts[1:]

        cot_slots = jnp.concatenate(parts, axis=1)

        def cot_for(step):
            place = (far + step) % n_far
            start = (place // per_half - x) % n_local * half + place % per_half * columns
            return lax.dynamic_slice_in_dim(cot_slots, start, columns, axis=1)

        came = [move(shift, cot_for(n_far - e), n_far - e) for e in range(1, n_far)]
        cot_rows = jnp.concatenate([cot_for(0)] + came, axis=0)
        fence = came + [weight_side, hidden[1]]

        for j in range(2, n_far):
            waits = gather_hop(0, j)
            if j == 2:
                weights[0] = weight_columns(0, weight_side)
                weight_side = move(swap, down_weight[middle:], 2)
                terms[0] = reduce_terms(0)
                waits += [terms[0][last_hop]]
            if j == last_hop:
                waits += reduce_hop(0, 1) + [weight_side]
            fence = waits

        waits = gather_hop(1, 1)
        weights[1] = weight_columns(1, weight_side)
        terms[1] = reduce_terms(1)
        rows[0] = gathered_rows(0)
        grads[0] = grad_terms(0)
        fence = waits + [terms[1][last_hop], grads[0][1]]

        for j in range(2, n_far):
            waits = gather_hop(1, j)
            if j == 2:
                waits += reduce_hop(1, 1)
                grad_side = move(swap, grads[0][1], 2)
                out_sums[0] = jnp.dot(rows[0], weights[0], preferred_element_type=jnp.float32)
                waits += [out_sums[0]]
            else:
                waits += reduce_hop(0, j - 1)
            if j == last_hop:
                waits += [grad_side]
            fence = waits
        grad_parts = [grads[0][0] + grad_side.astype(jnp.float32)]

        waits = reduce_hop(1, 2)
        rows[1] = gathered_rows(1)
        grads[1] = grad_terms(1)
        out_terms = (
            out_sums[0] + jnp.dot(rows[1], weights[1], preferred_element_type=jnp.float32)
        ).astype(jnp.bfloat16)
        fence = waits + [grads[1][1], out_terms]

        waits = reduce_hop(0, last_hop)
        grad_side = move(swap, grads[1][1], 2)
        outs = [out_terms[:tokens]] + [
            move(shift, out_terms[e * tokens : (e + 1) * tokens], e) for e in range(1, n_far)
        ]
        fence = waits + outs[1:]

        up_parts, gate_parts = [], []

        def reduced(f):
            up, down = travel["R", f]
            hidden_grad = terms[f][0] + up.astype(jnp.float32) + down.astype(jnp.float32)
            gate_wide, up_wide, sigmoid_gate = wide[f]
            up_parts.append((hidden_grad * gate_wide * sigmoid_gate).astype(jnp.bfloat16))
            gate_parts.append(
                (
                    hidden_grad * up_wide * sigmoid_gate * (1.0 + gate_wide * (1.0 - sigmoid_gate))
                ).astype(jnp.bfloat16)
            )

        reduced(0)
        out_slots = jnp.concatenate(outs, axis=1)

        def half_of(step):
            first = (x + step) % n_local * per_half
            starts = [(far - first - q) % n_far * columns for q in range(per_half)]
            return jnp.concatenate(
                [lax.dynamic_slice_in_dim(out_slots, s, columns, axis=1) for s in starts], axis=1
            )

        for j in range(3, n_far):
            waits = reduce_hop(1, j)
            if j == 3:
                sides = [move(local_shift, half_of(step), step) for step in range(1, n_local)]
            fence = waits
        reduced(1)
        output = half_of(0).astype(jnp.float32)
        for side in sides:
            output = output + side.astype(jnp.float32)
        output = output.astype(jnp.bfloat16).reshape(tokens, per_half, QUAD, width)
        grad_parts.append(grads[1][0] + grad_side.astype(jnp.float32))
        return (
            picked(output, slot_of(near), 2).reshape(tokens, half),
            jnp.concatenate(gate_parts, axis=1),
            jnp.concatenate(up_parts, axis=1),
            jnp.concatenate(grad_parts, axis=0),
        )

    specs = (P("hst", "local"), P("hst", "local"), P("hst", "local"), P("local", "hst"))
    return jax.shard_map(
        on_device, mesh=mesh, in_specs=specs, out_specs=specs, check_vma=False
    )
```

```python
import jax
import jax.numpy as jnp
from jax import lax
from jax.sharding import PartitionSpec as P

QUAD = 4
ORDER = (0, 2, 1, 3)
KEEP_COLS = (((1,), (1,)), ((), ()))
SUM_ROWS = (((0,), (0,)), ((), ()))


def after(value, *others):
    return lax.optimization_barrier((value,) + others)[0] if others else value


def slot_of(near):
    return [((near ^ block) & 1) << 1 | (near ^ block) >> 1 for block in range(QUAD)]


def picked(view, places, axis):
    return jnp.concatenate(
        [lax.dynamic_slice_in_dim(view, place, 1, axis=axis) for place in places], axis=axis
    )


def solution(mesh):
    n_hst, n_local = mesh.shape["hst"], mesh.shape["local"]
    n_far = n_hst // QUAD
    last_hop = n_far - 1

    def swap(value, bit):
        return lax.ppermute(value, "hst", [(h, h ^ bit) for h in range(n_hst)])

    def shift(value, step):
        pairs = [(h, (h + step * QUAD) % n_hst) for h in range(n_hst)]
        return lax.ppermute(value, "hst", pairs)

    def far_permute(value, pairs):
        pairs = [(s * QUAD + q, t * QUAD + q) for s, t in pairs for q in range(QUAD)]
        return lax.ppermute(value, "hst", pairs)

    def both_ways(up, down, sources):
        return (
            far_permute(up, [(z, z + 1) for z in sources]),
            far_permute(down, [(n_far - 1 - z, n_far - 2 - z) for z in sources]),
        )

    def local_shift(value, step):
        return lax.ppermute(value, "local", [(i, (i + step) % n_local) for i in range(n_local)])

    def on_device(gate_act, up_act, cotangent, down_weight):
        h = lax.axis_index("hst")
        x = lax.axis_index("local")
        far, near = h // QUAD, h % QUAD
        tokens, half = cotangent.shape
        width = down_weight.shape[1]
        columns = QUAD * width
        hidden_units = gate_act.shape[1]
        per_half = half // columns
        middle = 128 * ((hidden_units // 128 + 1) // 2)
        bounds = [(0, middle), (middle, hidden_units)]

        fence = []

        def move(send, value, *args):
            return send(after(value, *fence), *args)

        gate_all, up_all = gate_act.astype(jnp.float32), up_act.astype(jnp.float32)
        hidden = (gate_all * jax.nn.sigmoid(gate_all) * up_all).astype(jnp.bfloat16)
        lower = far < n_far // 2

        above, below, travel = {}, {}, {}

        def gather_hop(j):
            up, down = (below[j - 1], above[j - 1]) if j > 1 else (hidden, hidden)
            if j == last_hop:
                one = after(jnp.where(lower, down, up), *fence)
                ends = [(n_far - 2, n_far - 1), (1, 0)]
                below[j] = above[j] = far_permute(one, ends)
                return [below[j]]
            up, down = after(up, *fence), after(down, *fence)
            below[j], above[j] = both_ways(up, down, range(j - 1, n_far - 1))
            return [below[j], above[j]]

        def reduce_hop(f, j):
            d = n_far - j
            up_term, down_term = terms[f][d], terms[f][n_far - d]
            if j == 1:
                one = after(jnp.where(lower, up_term, down_term).astype(jnp.bfloat16), *fence)
                one = far_permute(one, [(0, 1), (n_far - 1, n_far - 2)])
                none = jnp.zeros_like(one)
                travel[f] = jnp.where(lower, one, none), jnp.where(lower, none, one)
                return [one]
            up, down = travel[f]
            up_term = (up_term + up.astype(jnp.float32)).astype(jnp.bfloat16)
            down_term = (down_term + down.astype(jnp.float32)).astype(jnp.bfloat16)
            up_term, down_term = after(up_term, *fence), after(down_term, *fence)
            travel[f] = both_ways(up_term, down_term, range(0, j))
            return list(travel[f])

        def weight_columns(f, other):
            lo, hi = bounds[f]
            pair = jnp.concatenate([down_weight[lo:hi], other], axis=1)
            return jnp.concatenate([pair, move(swap, pair, 1)], axis=1)

        def reduce_terms(f):
            dots = lax.dot_general(
                cot_rows, weights[f], KEEP_COLS, preferred_element_type=jnp.float32
            )
            return [dots[e * tokens : (e + 1) * tokens] for e in range(n_far)]

        def gathered_rows(f):
            lo, hi = bounds[f]
            slots = [hidden[:, lo:hi]]
            for e in range(1, n_far):
                above_e, below_e = after(above[e], *fence), after(below[n_far - e], *fence)
                slots.append(jnp.where(far + e < n_far, above_e[:, lo:hi], below_e[:, lo:hi]))
            return jnp.concatenate(slots, axis=0)

        core_sides = []

        def grad_terms(f):
            keep, give = (
                lax.dot_general(rows[f], part, SUM_ROWS, preferred_element_type=jnp.float32)
                for part in (cot_rows[:, : 2 * width], cot_rows[:, 2 * width :])
            )
            theirs = move(swap, after(give.astype(jnp.bfloat16), *core_sides), 1)
            core_sides[:] = [theirs]
            return (
                keep[:, :width] + theirs[:, :width].astype(jnp.float32),
                (keep[:, width:] + theirs[:, width:].astype(jnp.float32)).astype(jnp.bfloat16),
            )

        weights, terms, rows = {}, {}, {}

        parts = [cotangent] + [local_shift(cotangent, n_local - s) for s in range(1, n_local)]
        weight_side = swap(down_weight[:middle], 2)
        waits = gather_hop(1)
        cot_slots = jnp.concatenate(parts, axis=1).reshape(tokens, n_far, QUAD, width)
        cot_slots = picked(cot_slots, [near ^ k for k in ORDER], 2).reshape(tokens, n_far, columns)

        def cot_for(step):
            place = (far + step) % n_far
            start = (place // per_half - x) % n_local * per_half + place % per_half
            return lax.dynamic_index_in_dim(cot_slots, start, axis=1, keepdims=False)

        came = [shift(cot_for(n_far - e), n_far - e) for e in range(1, n_far)]
        cot_rows = jnp.concatenate([cot_for(0)] + came, axis=0)
        fence = waits + came + [weight_side]

        for j in range(2, n_far):
            waits = gather_hop(j)
            if j == 2:
                weights[0] = weight_columns(0, weight_side)
                weight_side = move(swap, down_weight[middle:], 2)
                terms[0] = reduce_terms(0)
                waits.append(weight_side)
            waits += reduce_hop(0, j - 1)
            if j == 3:
                weights[1] = weight_columns(1, weight_side)
                terms[1] = reduce_terms(1)
            if j > 2:
                waits += reduce_hop(1, j - 2)
            fence = waits

        waits = reduce_hop(0, last_hop) + reduce_hop(1, last_hop - 1)
        out_sum, grad_parts, grad_side = 0.0, [], None
        for f in range(2):
            rows[f] = gathered_rows(f)
            mine, give = grad_terms(f)
            waits.append(give)
            give = give if grad_side is None else after(give, grad_side)
            grad_side = move(swap, give, 2)
            grad_parts.append(mine + grad_side.astype(jnp.float32))
            out_sum += jnp.dot(rows[f], weights[f], preferred_element_type=jnp.float32)
        out_terms = out_sum.astype(jnp.bfloat16)
        fence = waits + [out_terms]

        waits = reduce_hop(1, last_hop)
        outs = [out_terms[:tokens]] + [
            move(shift, out_terms[e * tokens : (e + 1) * tokens], e) for e in range(1, n_far)
        ]
        up_parts, gate_parts = [], []
        for f in range(2):
            up, down = travel[f]
            hidden_grad = terms[f][0] + up.astype(jnp.float32) + down.astype(jnp.float32)
            lo, hi = bounds[f]
            gate_wide = gate_act[:, lo:hi].astype(jnp.float32)
            up_wide = up_act[:, lo:hi].astype(jnp.float32)
            sigmoid_gate = jax.nn.sigmoid(gate_wide)
            up_parts.append((hidden_grad * gate_wide * sigmoid_gate).astype(jnp.bfloat16))
            gate_parts.append(
                (
                    hidden_grad * up_wide * sigmoid_gate * (1.0 + gate_wide * (1.0 - sigmoid_gate))
                ).astype(jnp.bfloat16)
            )

        out_slots = jnp.concatenate(outs, axis=1)

        def half_of(step):
            first = (x + step) % n_local * per_half
            starts = [(far - first - q) % n_far * columns for q in range(per_half)]
            return jnp.concatenate(
                [lax.dynamic_slice_in_dim(out_slots, s, columns, axis=1) for s in starts], axis=1
            )

        sides = [local_shift(half_of(step), step) for step in range(1, n_local)]
        output = half_of(0).astype(jnp.float32)
        for side in sides:
            output = output + side.astype(jnp.float32)
        output = output.astype(jnp.bfloat16).reshape(tokens, per_half, QUAD, width)
        return (
            picked(output, slot_of(near), 2).reshape(tokens, half),
            jnp.concatenate(gate_parts, axis=1),
            jnp.concatenate(up_parts, axis=1),
            jnp.concatenate(grad_parts, axis=0),
        )

    specs = (P("hst", "local"), P("hst", "local"), P("hst", "local"), P("local", "hst"))
    return jax.shard_map(
        on_device, mesh=mesh, in_specs=specs, out_specs=specs, check_vma=False
    )
```

```python
import jax
import jax.numpy as jnp
from jax import lax
from jax.sharding import PartitionSpec as P

QUAD = 4
ORDER = (0, 2, 1, 3)
KEEP_COLS = (((1,), (1,)), ((), ()))
SUM_ROWS = (((0,), (0,)), ((), ()))


def after(value, *others):
    return lax.optimization_barrier((value,) + others)[0] if others else value


def slot_of(near):
    return [((near ^ block) & 1) << 1 | (near ^ block) >> 1 for block in range(QUAD)]


def picked(view, places, axis):
    return jnp.concatenate(
        [lax.dynamic_slice_in_dim(view, place, 1, axis=axis) for place in places], axis=axis
    )


def solution(mesh):
    n_hst, n_local = mesh.shape["hst"], mesh.shape["local"]
    n_far = n_hst // QUAD
    last_hop = n_far - 1

    def swap(value, bit):
        return lax.ppermute(value, "hst", [(h, h ^ bit) for h in range(n_hst)])

    def shift(value, step):
        pairs = [(h, (h + step * QUAD) % n_hst) for h in range(n_hst)]
        return lax.ppermute(value, "hst", pairs)

    def far_permute(value, pairs):
        pairs = [(s * QUAD + q, t * QUAD + q) for s, t in pairs for q in range(QUAD)]
        return lax.ppermute(value, "hst", pairs)

    def both_ways(up, down, sources):
        return (
            far_permute(up, [(z, z + 1) for z in sources]),
            far_permute(down, [(n_far - 1 - z, n_far - 2 - z) for z in sources]),
        )

    def local_shift(value, step):
        return lax.ppermute(value, "local", [(i, (i + step) % n_local) for i in range(n_local)])

    def on_device(gate_act, up_act, cotangent, down_weight):
        h = lax.axis_index("hst")
        x = lax.axis_index("local")
        far, near = h // QUAD, h % QUAD
        tokens, half = cotangent.shape
        width = down_weight.shape[1]
        columns = QUAD * width
        hidden_units = gate_act.shape[1]
        per_half = half // columns
        middle = 128 * ((hidden_units // 128 + 1) // 2)
        bounds = [(0, middle), (middle, hidden_units)]

        fence = []

        def move(send, value, *args):
            return send(after(value, *fence), *args)

        gate_all, up_all = gate_act.astype(jnp.float32), up_act.astype(jnp.float32)
        hidden = (gate_all * jax.nn.sigmoid(gate_all) * up_all).astype(jnp.bfloat16)
        lower = far < n_far // 2

        above, below, travel = {}, {}, {}

        def gather_hop(j):
            up, down = (below[j - 1], above[j - 1]) if j > 1 else (hidden, hidden)
            if j == last_hop:
                one = after(jnp.where(lower, down, up), *fence)
                ends = [(n_far - 2, n_far - 1), (1, 0)]
                below[j] = above[j] = far_permute(one, ends)
                return [below[j]]
            up, down = after(up, *fence), after(down, *fence)
            below[j], above[j] = both_ways(up, down, range(j - 1, n_far - 1))
            return [below[j], above[j]]

        def reduce_hop(f, j):
            d = n_far - j
            up_term, down_term = terms[f][d], terms[f][n_far - d]
            if j == 1:
                one = after(jnp.where(lower, up_term, down_term).astype(jnp.bfloat16), *fence)
                one = far_permute(one, [(0, 1), (n_far - 1, n_far - 2)])
                none = jnp.zeros_like(one)
                travel[f] = jnp.where(lower, one, none), jnp.where(lower, none, one)
                return [one]
            up, down = travel[f]
            up_term = (up_term + up.astype(jnp.float32)).astype(jnp.bfloat16)
            down_term = (down_term + down.astype(jnp.float32)).astype(jnp.bfloat16)
            up_term, down_term = after(up_term, *fence), after(down_term, *fence)
            travel[f] = both_ways(up_term, down_term, range(0, j))
            return list(travel[f])

        def weight_columns(f, other):
            lo, hi = bounds[f]
            pair = jnp.concatenate([down_weight[lo:hi], other], axis=1)
            return jnp.concatenate([pair, move(swap, pair, 1)], axis=1)

        def reduce_terms(f):
            dots = lax.dot_general(
                cot_rows, weights[f], KEEP_COLS, preferred_element_type=jnp.float32
            )
            return [dots[e * tokens : (e + 1) * tokens] for e in range(n_far)]

        def gathered_rows(f):
            lo, hi = bounds[f]
            slots = [after(hidden, *fence)[:, lo:hi]]
            for e in range(1, n_far):
                above_e, below_e = after(above[e], *fence), after(below[n_far - e], *fence)
                slots.append(jnp.where(far + e < n_far, above_e[:, lo:hi], below_e[:, lo:hi]))
            return jnp.concatenate(slots, axis=0)

        core_sides = []

        def grad_terms(f):
            keep, give = (
                lax.dot_general(rows[f], part, SUM_ROWS, preferred_element_type=jnp.float32)
                for part in (cot_rows[:, : 2 * width], cot_rows[:, 2 * width :])
            )
            theirs = move(swap, after(give.astype(jnp.bfloat16), *core_sides), 1)
            core_sides[:] = [theirs]
            return (
                keep[:, :width] + theirs[:, :width].astype(jnp.float32),
                (keep[:, width:] + theirs[:, width:].astype(jnp.float32)).astype(jnp.bfloat16),
            )

        weights, terms, rows = {}, {}, {}

        parts = [cotangent] + [local_shift(cotangent, n_local - s) for s in range(1, n_local)]
        weight_side = swap(down_weight[:middle], 2)
        waits = gather_hop(1)
        cot_slots = jnp.concatenate(parts, axis=1).reshape(tokens, n_far, QUAD, width)
        cot_slots = picked(cot_slots, [near ^ k for k in ORDER], 2).reshape(tokens, n_far, columns)

        def cot_for(step):
            place = (far + step) % n_far
            start = (place // per_half - x) % n_local * per_half + place % per_half
            return lax.dynamic_index_in_dim(cot_slots, start, axis=1, keepdims=False)

        came = []
        for e in range(1, n_far):
            came.append(shift(after(cot_for(n_far - e), *came[: max(0, e - 2)]), n_far - e))
        cot_rows = jnp.concatenate([cot_for(0)] + came, axis=0)
        fence = waits + came + [weight_side]

        for j in range(2, n_far):
            waits = gather_hop(j)
            if j == 2:
                weights[0] = weight_columns(0, weight_side)
                weight_side = move(swap, down_weight[middle:], 2)
                terms[0] = reduce_terms(0)
                waits.append(weight_side)
            waits += reduce_hop(0, j - 1)
            if j == 3:
                weights[1] = weight_columns(1, weight_side)
                terms[1] = reduce_terms(1)
            if j > 2:
                waits += reduce_hop(1, j - 2)
            fence = waits

        gather_fence, fence = fence, []
        waits = reduce_hop(0, last_hop) + reduce_hop(1, last_hop - 1)
        fence = gather_fence
        grad_parts, grad_side = [], None
        for f in range(2):
            fence = gather_fence + core_sides
            rows[f] = gathered_rows(f)
            mine, give = grad_terms(f)
            if f == 0:
                waits.append(give)
            give = give if grad_side is None else after(give, grad_side)
            grad_side = swap(give, 2)
            grad_parts.append(mine + grad_side.astype(jnp.float32))
        fence = waits

        fence = waits[:2] + waits[-1:]
        waits, before = reduce_hop(1, last_hop), waits
        fence = before
        out_sum = 0.0
        for f in range(2):
            out_sum += jnp.dot(
                after(rows[f], *fence), weights[f], preferred_element_type=jnp.float32
            )
        out_terms = after(out_sum.astype(jnp.bfloat16), *waits)
        outs = [out_terms[:tokens]] + [
            shift(out_terms[e * tokens : (e + 1) * tokens], e) for e in range(1, n_far)
        ]
        up_parts, gate_parts = [], []
        for f in range(2):
            up, down = travel[f]
            hidden_grad = terms[f][0] + up.astype(jnp.float32) + down.astype(jnp.float32)
            lo, hi = bounds[f]
            gate_wide = gate_act[:, lo:hi].astype(jnp.float32)
            up_wide = up_act[:, lo:hi].astype(jnp.float32)
            sigmoid_gate = jax.nn.sigmoid(gate_wide)
            up_parts.append((hidden_grad * gate_wide * sigmoid_gate).astype(jnp.bfloat16))
            gate_parts.append(
                (
                    hidden_grad * up_wide * sigmoid_gate * (1.0 + gate_wide * (1.0 - sigmoid_gate))
                ).astype(jnp.bfloat16)
            )

        out_slots = jnp.concatenate(outs, axis=1)

        def half_of(step):
            first = (x + step) % n_local * per_half
            starts = [(far - first - q) % n_far * columns for q in range(per_half)]
            return jnp.concatenate(
                [lax.dynamic_slice_in_dim(out_slots, s, columns, axis=1) for s in starts], axis=1
            )

        sides = [local_shift(half_of(step), step) for step in range(1, n_local)]
        output = half_of(0).astype(jnp.float32)
        for side in sides:
            output = output + side.astype(jnp.float32)
        output = output.astype(jnp.bfloat16).reshape(tokens, per_half, QUAD, width)
        return (
            picked(output, slot_of(near), 2).reshape(tokens, half),
            jnp.concatenate(gate_parts, axis=1),
            jnp.concatenate(up_parts, axis=1),
            jnp.concatenate(grad_parts, axis=0),
        )

    specs = (P("hst", "local"), P("hst", "local"), P("hst", "local"), P("local", "hst"))
    return jax.shard_map(
        on_device, mesh=mesh, in_specs=specs, out_specs=specs, check_vma=False
    )
```

```python
import jax
import jax.numpy as jnp
from jax import lax
from jax.sharding import PartitionSpec as P

QUAD = 4
ORDER = (0, 2, 1, 3)
KEEP_COLS = (((1,), (1,)), ((), ()))
SUM_ROWS = (((0,), (0,)), ((), ()))


def after(value, *others):
    return lax.optimization_barrier((value,) + others)[0] if others else value


def slot_of(near):
    return [((near ^ block) & 1) << 1 | (near ^ block) >> 1 for block in range(QUAD)]


def picked(view, places, axis):
    return jnp.concatenate(
        [lax.dynamic_slice_in_dim(view, place, 1, axis=axis) for place in places], axis=axis
    )


def solution(mesh):
    n_hst, n_local = mesh.shape["hst"], mesh.shape["local"]
    n_far = n_hst // QUAD
    last_hop = n_far - 1

    def swap(value, bit):
        return lax.ppermute(value, "hst", [(h, h ^ bit) for h in range(n_hst)])

    def shift(value, step):
        pairs = [(h, (h + step * QUAD) % n_hst) for h in range(n_hst)]
        return lax.ppermute(value, "hst", pairs)

    def far_permute(value, pairs):
        pairs = [(s * QUAD + q, t * QUAD + q) for s, t in pairs for q in range(QUAD)]
        return lax.ppermute(value, "hst", pairs)

    def both_ways(up, down, sources):
        return (
            far_permute(up, [(z, z + 1) for z in sources]),
            far_permute(down, [(n_far - 1 - z, n_far - 2 - z) for z in sources]),
        )

    def local_shift(value, step):
        return lax.ppermute(value, "local", [(i, (i + step) % n_local) for i in range(n_local)])

    def on_device(gate_act, up_act, cotangent, down_weight):
        h = lax.axis_index("hst")
        x = lax.axis_index("local")
        far, near = h // QUAD, h % QUAD
        tokens, half = cotangent.shape
        width = down_weight.shape[1]
        columns = QUAD * width
        hidden_units = gate_act.shape[1]
        per_half = half // columns
        middle = 128 * ((hidden_units // 128 + 1) // 2)
        bounds = [(0, middle), (middle, hidden_units)]

        fence = []

        def move(send, value, *args):
            return send(after(value, *fence), *args)

        gate_all, up_all = gate_act.astype(jnp.float32), up_act.astype(jnp.float32)
        hidden = (gate_all * jax.nn.sigmoid(gate_all) * up_all).astype(jnp.bfloat16)
        lower = far < n_far // 2

        above, below, travel = {}, {}, {}

        def gather_hop(j):
            up, down = (below[j - 1], above[j - 1]) if j > 1 else (hidden, hidden)
            if j == last_hop:
                one = after(jnp.where(lower, down, up), *fence)
                ends = [(n_far - 2, n_far - 1), (1, 0)]
                below[j] = above[j] = far_permute(one, ends)
                return [below[j]]
            up, down = after(up, *fence), after(down, *fence)
            below[j], above[j] = both_ways(up, down, range(j - 1, n_far - 1))
            return [below[j], above[j]]

        def reduce_hop(f, j):
            d = n_far - j
            up_term, down_term = terms[f][d], terms[f][n_far - d]
            if j == 1:
                one = after(jnp.where(lower, up_term, down_term).astype(jnp.bfloat16), *fence)
                one = far_permute(one, [(0, 1), (n_far - 1, n_far - 2)])
                none = jnp.zeros_like(one)
                travel[f] = jnp.where(lower, one, none), jnp.where(lower, none, one)
                return [one]
            up, down = travel[f]
            up_term = (up_term + up.astype(jnp.float32)).astype(jnp.bfloat16)
            down_term = (down_term + down.astype(jnp.float32)).astype(jnp.bfloat16)
            up_term, down_term = after(up_term, *fence), after(down_term, *fence)
            travel[f] = both_ways(up_term, down_term, range(0, j))
            return list(travel[f])

        def weight_columns(f, other):
            lo, hi = bounds[f]
            pair = jnp.concatenate([down_weight[lo:hi], other], axis=1)
            return jnp.concatenate([pair, move(swap, pair, 1)], axis=1)

        def reduce_terms(f):
            dots = lax.dot_general(
                cot_rows, weights[f], KEEP_COLS, preferred_element_type=jnp.float32
            )
            return [dots[e * tokens : (e + 1) * tokens] for e in range(n_far)]

        def gathered_rows(f):
            lo, hi = bounds[f]
            slots = [after(hidden, *fence)[:, lo:hi]]
            for e in range(1, n_far):
                above_e, below_e = after(above[e], *fence), after(below[n_far - e], *fence)
                slots.append(jnp.where(far + e < n_far, above_e[:, lo:hi], below_e[:, lo:hi]))
            return jnp.concatenate(slots, axis=0)

        core_sides = []

        def grad_terms(f):
            keep, give = (
                lax.dot_general(rows[f], part, SUM_ROWS, preferred_element_type=jnp.float32)
                for part in (cot_rows[:, : 2 * width], cot_rows[:, 2 * width :])
            )
            theirs = move(swap, after(give.astype(jnp.bfloat16), *core_sides), 1)
            core_sides[:] = [theirs]
            return (
                keep[:, :width] + theirs[:, :width].astype(jnp.float32),
                (keep[:, width:] + theirs[:, width:].astype(jnp.float32)).astype(jnp.bfloat16),
            )

        weights, terms, rows = {}, {}, {}

        parts = [cotangent] + [local_shift(cotangent, n_local - s) for s in range(1, n_local)]
        weight_side = swap(down_weight[:middle], 2)
        waits = gather_hop(1)
        cot_slots = jnp.concatenate(parts, axis=1).reshape(tokens, n_far, QUAD, width)
        cot_slots = picked(cot_slots, [near ^ k for k in ORDER], 2).reshape(tokens, n_far, columns)

        def cot_for(step):
            place = (far + step) % n_far
            start = (place // per_half - x) % n_local * per_half + place % per_half
            return lax.dynamic_index_in_dim(cot_slots, start, axis=1, keepdims=False)

        came = []
        for e in range(1, n_far):
            came.append(shift(after(cot_for(n_far - e), *came[: max(0, e - 2)]), n_far - e))
        cot_rows = jnp.concatenate([cot_for(0)] + came, axis=0)
        fence = waits + came + [weight_side]

        for j in range(2, n_far):
            waits = gather_hop(j)
            if j == 2:
                weights[0] = weight_columns(0, weight_side)
                weight_side = move(swap, down_weight[middle:], 2)
                terms[0] = reduce_terms(0)
                waits.append(weight_side)
            waits += reduce_hop(0, j - 1)
            if j == 3:
                weights[1] = weight_columns(1, weight_side)
                terms[1] = reduce_terms(1)
            if j > 2:
                waits += reduce_hop(1, j - 2)
            fence = waits

        gather_fence = fence
        waits = reduce_hop(0, last_hop) + reduce_hop(1, last_hop - 1)
        grad_parts = []
        for f in range(2):
            fence = gather_fence + (waits[-1:] if f else [])
            rows[f] = gathered_rows(f)
            mine, give = grad_terms(f)
            if f == 0:
                waits.append(give)
                for part in travel:
                    travel[part] = tuple(after(value, give) for value in travel[part])
            grad_side = swap(give, 2)
            grad_parts.append(mine + grad_side.astype(jnp.float32))
        fence = waits

        fence = waits[:2] + waits[-1:]
        waits, before = reduce_hop(1, last_hop), waits
        fence = before
        out_sum = 0.0
        for f in range(2):
            out_sum += jnp.dot(
                after(rows[f], *fence), weights[f], preferred_element_type=jnp.float32
            )
        out_terms = after(out_sum.astype(jnp.bfloat16), *waits)
        outs = [out_terms[:tokens]]
        for e in range(1, n_far):
            term = out_terms[e * tokens : (e + 1) * tokens]
            outs.append(shift(after(term, *outs[1 : max(1, e - 1)]), e))
        up_parts, gate_parts = [], []
        for f in range(2):
            up, down = travel[f]
            hidden_grad = terms[f][0] + up.astype(jnp.float32) + down.astype(jnp.float32)
            lo, hi = bounds[f]
            gate_wide = gate_act[:, lo:hi].astype(jnp.float32)
            up_wide = up_act[:, lo:hi].astype(jnp.float32)
            sigmoid_gate = jax.nn.sigmoid(gate_wide)
            up_parts.append((hidden_grad * gate_wide * sigmoid_gate).astype(jnp.bfloat16))
            gate_parts.append(
                (
                    hidden_grad * up_wide * sigmoid_gate * (1.0 + gate_wide * (1.0 - sigmoid_gate))
                ).astype(jnp.bfloat16)
            )

        out_slots = jnp.concatenate(outs, axis=1)

        def half_of(step):
            first = (x + step) % n_local * per_half
            starts = [(far - first - q) % n_far * columns for q in range(per_half)]
            return jnp.concatenate(
                [lax.dynamic_slice_in_dim(out_slots, s, columns, axis=1) for s in starts], axis=1
            )

        sides = [local_shift(half_of(step), step) for step in range(1, n_local)]
        output = half_of(0).astype(jnp.float32)
        for side in sides:
            output = output + side.astype(jnp.float32)
        output = output.astype(jnp.bfloat16).reshape(tokens, per_half, QUAD, width)
        return (
            picked(output, slot_of(near), 2).reshape(tokens, half),
            jnp.concatenate(gate_parts, axis=1),
            jnp.concatenate(up_parts, axis=1),
            jnp.concatenate(grad_parts, axis=0),
        )

    specs = (P("hst", "local"), P("hst", "local"), P("hst", "local"), P("local", "hst"))
    return jax.shard_map(
        on_device, mesh=mesh, in_specs=specs, out_specs=specs, check_vma=False
    )
```

```python
import jax
import jax.numpy as jnp
from jax import lax
from jax.sharding import PartitionSpec as P

QUAD = 4
ORDER = (0, 2, 1, 3)
KEEP_COLS = (((1,), (1,)), ((), ()))
SUM_ROWS = (((0,), (0,)), ((), ()))


def after(value, *others):
    return lax.optimization_barrier((value,) + others)[0] if others else value


def slot_of(near):
    return [((near ^ block) & 1) << 1 | (near ^ block) >> 1 for block in range(QUAD)]


def picked(view, places, axis):
    return jnp.concatenate(
        [lax.dynamic_slice_in_dim(view, place, 1, axis=axis) for place in places], axis=axis
    )


def solution(mesh):
    n_hst, n_local = mesh.shape["hst"], mesh.shape["local"]
    n_far = n_hst // QUAD
    last_hop = n_far - 1

    def swap(value, bit):
        return lax.ppermute(value, "hst", [(h, h ^ bit) for h in range(n_hst)])

    def shift(value, step):
        pairs = [(h, (h + step * QUAD) % n_hst) for h in range(n_hst)]
        return lax.ppermute(value, "hst", pairs)

    def far_permute(value, pairs):
        pairs = [(s * QUAD + q, t * QUAD + q) for s, t in pairs for q in range(QUAD)]
        return lax.ppermute(value, "hst", pairs)

    def both_ways(up, down, sources):
        return (
            far_permute(up, [(z, z + 1) for z in sources]),
            far_permute(down, [(n_far - 1 - z, n_far - 2 - z) for z in sources]),
        )

    def local_shift(value, step):
        return lax.ppermute(value, "local", [(i, (i + step) % n_local) for i in range(n_local)])

    def on_device(gate_act, up_act, cotangent, down_weight):
        h = lax.axis_index("hst")
        x = lax.axis_index("local")
        far, near = h // QUAD, h % QUAD
        tokens, half = cotangent.shape
        width = down_weight.shape[1]
        columns = QUAD * width
        hidden_units = gate_act.shape[1]
        per_half = half // columns
        middle = 128 * ((hidden_units // 128 + 1) // 2)
        bounds = [(0, middle), (middle, hidden_units)]

        fence = []

        def move(send, value, *args):
            return send(after(value, *fence), *args)

        gate_all, up_all = gate_act.astype(jnp.float32), up_act.astype(jnp.float32)
        hidden = (gate_all * jax.nn.sigmoid(gate_all) * up_all).astype(jnp.bfloat16)
        lower = far < n_far // 2

        above, below, travel = {}, {}, {}

        def gather_hop(j):
            up, down = (below[j - 1], above[j - 1]) if j > 1 else (hidden, hidden)
            if j == last_hop:
                one = after(jnp.where(lower, down, up), *fence)
                ends = [(n_far - 2, n_far - 1), (1, 0)]
                below[j] = above[j] = far_permute(one, ends)
                return [below[j]]
            up, down = after(up, *fence), after(down, *fence)
            below[j], above[j] = both_ways(up, down, range(j - 1, n_far - 1))
            return [below[j], above[j]]

        def reduce_hop(f, j):
            d = n_far - j
            up_term, down_term = terms[f][d], terms[f][n_far - d]
            if j == 1:
                one = after(jnp.where(lower, up_term, down_term).astype(jnp.bfloat16), *fence)
                one = far_permute(one, [(0, 1), (n_far - 1, n_far - 2)])
                none = jnp.zeros_like(one)
                travel[f] = jnp.where(lower, one, none), jnp.where(lower, none, one)
                return [one]
            up, down = travel[f]
            up_term = (up_term + up.astype(jnp.float32)).astype(jnp.bfloat16)
            down_term = (down_term + down.astype(jnp.float32)).astype(jnp.bfloat16)
            up_term, down_term = after(up_term, *fence), after(down_term, *fence)
            travel[f] = both_ways(up_term, down_term, range(0, j))
            return list(travel[f])

        def weight_columns(f, other):
            lo, hi = bounds[f]
            pair = jnp.concatenate([down_weight[lo:hi], other], axis=1)
            return jnp.concatenate([pair, move(swap, pair, 1)], axis=1)

        def reduce_terms(f):
            dots = lax.dot_general(
                cot_rows, weights[f], KEEP_COLS, preferred_element_type=jnp.float32
            )
            return [dots[e * tokens : (e + 1) * tokens] for e in range(n_far)]

        weights, terms = {}, {}

        parts = [cotangent] + [local_shift(cotangent, n_local - s) for s in range(1, n_local)]
        weight_side = swap(down_weight[:middle], 2)
        waits = gather_hop(1)
        cot_slots = jnp.concatenate(parts, axis=1).reshape(tokens, n_far, QUAD, width)
        cot_slots = picked(cot_slots, [near ^ k for k in ORDER], 2).reshape(tokens, n_far, columns)

        def cot_for(step):
            place = (far + step) % n_far
            start = (place // per_half - x) % n_local * per_half + place % per_half
            return lax.dynamic_index_in_dim(cot_slots, start, axis=1, keepdims=False)

        came = []
        for e in range(1, n_far):
            came.append(shift(after(cot_for(n_far - e), *came[: max(0, e - 2)]), n_far - e))
        cot_rows = jnp.concatenate([cot_for(0)] + came, axis=0)
        fence = waits + came + [weight_side]

        for j in range(2, n_far):
            waits = gather_hop(j)
            if j == 2:
                weights[0] = weight_columns(0, weight_side)
                weight_side = move(swap, down_weight[middle:], 2)
                terms[0] = reduce_terms(0)
                waits.append(weight_side)
            waits += reduce_hop(0, j - 1)
            if j == 3:
                weights[1] = weight_columns(1, weight_side)
                terms[1] = reduce_terms(1)
            if j > 2:
                waits += reduce_hop(1, j - 2)
            fence = waits

        gather_fence, fence = fence, []
        waits = reduce_hop(0, last_hop)
        fence = gather_fence
        waits += reduce_hop(1, last_hop - 1)
        slots = [after(hidden, *fence)]
        for e in range(1, n_far):
            above_e, below_e = after(above[e], *fence), after(below[n_far - e], *fence)
            slots.append(jnp.where(far + e < n_far, above_e, below_e))
        rows = jnp.concatenate(slots, axis=0)
        give, keep = (
            lax.dot_general(rows, part, SUM_ROWS, preferred_element_type=jnp.float32)
            for part in (cot_rows[:, 2 * width :], cot_rows[:, : 2 * width])
        )
        theirs = swap(give.astype(jnp.bfloat16), 1)
        give = (keep[:, width:] + theirs[:, width:].astype(jnp.float32)).astype(jnp.bfloat16)
        other_grad = swap(give, 2)
        for part in travel:
            travel[part] = tuple(after(value, give) for value in travel[part])
        grad = keep[:, :width] + theirs[:, :width].astype(jnp.float32)
        down_grad = grad + other_grad.astype(jnp.float32)

        fence = waits + [give]
        waits = reduce_hop(1, last_hop)
        rows = after(rows, *fence)
        out_sum = 0.0
        for f, (lo, hi) in enumerate(bounds):
            out_sum += jnp.dot(rows[:, lo:hi], weights[f], preferred_element_type=jnp.float32)
        out_terms = after(out_sum.astype(jnp.bfloat16), *waits)
        outs = [out_terms[:tokens]]
        for e in range(1, n_far):
            term = out_terms[e * tokens : (e + 1) * tokens]
            outs.append(shift(after(term, *outs[1 : max(1, e - 1)]), e))
        up_parts, gate_parts = [], []
        for f in range(2):
            up, down = travel[f]
            hidden_grad = terms[f][0] + up.astype(jnp.float32) + down.astype(jnp.float32)
            lo, hi = bounds[f]
            gate_wide = gate_act[:, lo:hi].astype(jnp.float32)
            up_wide = up_act[:, lo:hi].astype(jnp.float32)
            sigmoid_gate = jax.nn.sigmoid(gate_wide)
            up_parts.append((hidden_grad * gate_wide * sigmoid_gate).astype(jnp.bfloat16))
            gate_parts.append(
                (
                    hidden_grad * up_wide * sigmoid_gate * (1.0 + gate_wide * (1.0 - sigmoid_gate))
                ).astype(jnp.bfloat16)
            )

        out_slots = jnp.concatenate(outs, axis=1)

        def half_of(step):
            first = (x + step) % n_local * per_half
            starts = [(far - first - q) % n_far * columns for q in range(per_half)]
            return jnp.concatenate(
                [lax.dynamic_slice_in_dim(out_slots, s, columns, axis=1) for s in starts], axis=1
            )

        sides = [local_shift(half_of(step), step) for step in range(1, n_local)]
        output = half_of(0).astype(jnp.float32)
        for side in sides:
            output = output + side.astype(jnp.float32)
        output = output.astype(jnp.bfloat16).reshape(tokens, per_half, QUAD, width)
        return (
            picked(output, slot_of(near), 2).reshape(tokens, half),
            jnp.concatenate(gate_parts, axis=1),
            jnp.concatenate(up_parts, axis=1),
            down_grad,
        )

    specs = (P("hst", "local"), P("hst", "local"), P("hst", "local"), P("local", "hst"))
    return jax.shard_map(
        on_device, mesh=mesh, in_specs=specs, out_specs=specs, check_vma=False
    )
```

```python
import jax
import jax.numpy as jnp
from jax import lax
from jax.sharding import PartitionSpec as P

QUAD = 4
ORDER = (0, 2, 1, 3)
KEEP_COLS = (((1,), (1,)), ((), ()))
SUM_ROWS = (((0,), (0,)), ((), ()))


def after(value, *others):
    return lax.optimization_barrier((value,) + others)[0] if others else value


def slot_of(near):
    return [((near ^ block) & 1) << 1 | (near ^ block) >> 1 for block in range(QUAD)]


def picked(view, places, axis):
    return jnp.concatenate(
        [lax.dynamic_slice_in_dim(view, place, 1, axis=axis) for place in places], axis=axis
    )


def solution(mesh):
    n_hst, n_local = mesh.shape["hst"], mesh.shape["local"]
    n_far = n_hst // QUAD
    last_hop = n_far - 1

    def swap(value, bit):
        return lax.ppermute(value, "hst", [(h, h ^ bit) for h in range(n_hst)])

    def shift(value, step):
        pairs = [(h, (h + step * QUAD) % n_hst) for h in range(n_hst)]
        return lax.ppermute(value, "hst", pairs)

    def far_permute(value, pairs):
        pairs = [(s * QUAD + q, t * QUAD + q) for s, t in pairs for q in range(QUAD)]
        return lax.ppermute(value, "hst", pairs)

    def both_ways(up, down, sources):
        return (
            far_permute(up, [(z, z + 1) for z in sources]),
            far_permute(down, [(n_far - 1 - z, n_far - 2 - z) for z in sources]),
        )

    def local_shift(value, step):
        return lax.ppermute(value, "local", [(i, (i + step) % n_local) for i in range(n_local)])

    def on_device(gate_act, up_act, cotangent, down_weight):
        h = lax.axis_index("hst")
        x = lax.axis_index("local")
        far, near = h // QUAD, h % QUAD
        tokens, half = cotangent.shape
        width = down_weight.shape[1]
        columns = QUAD * width
        hidden_units = gate_act.shape[1]
        per_half = half // columns
        middle = 128 * ((hidden_units // 128 + 1) // 2)
        bounds = [(0, middle), (middle, hidden_units)]

        fence = []

        def move(send, value, *args):
            return send(after(value, *fence), *args)

        hidden = []
        for lo, hi in bounds:
            gate_wide = gate_act[:, lo:hi].astype(jnp.float32)
            up_wide = up_act[:, lo:hi].astype(jnp.float32)
            hidden.append((gate_wide * jax.nn.sigmoid(gate_wide) * up_wide).astype(jnp.bfloat16))
        lower = far < n_far // 2

        above, below, travel = ({}, {}), ({}, {}), {}

        def gather_hop(f, j):
            up, down = (below[f][j - 1], above[f][j - 1]) if j > 1 else (hidden[f], hidden[f])
            if j == last_hop:
                one = after(jnp.where(lower, down, up), *fence)
                one = far_permute(one, [(n_far - 2, n_far - 1), (1, 0)])
                below[f][j] = above[f][j] = one
                return [one]
            up, down = after(up, *fence), after(down, *fence)
            below[f][j], above[f][j] = both_ways(up, down, range(j - 1, n_far - 1))
            return [below[f][j], above[f][j]]

        def reduce_hop(f, j):
            d = n_far - j
            up_term, down_term = terms[f][d], terms[f][n_far - d]
            if j == 1:
                one = after(jnp.where(lower, up_term, down_term).astype(jnp.bfloat16), *fence)
                one = far_permute(one, [(0, 1), (n_far - 1, n_far - 2)])
                none = jnp.zeros_like(one)
                travel[f] = jnp.where(lower, one, none), jnp.where(lower, none, one)
                return [one]
            up, down = travel[f]
            up_term = (up_term + up.astype(jnp.float32)).astype(jnp.bfloat16)
            down_term = (down_term + down.astype(jnp.float32)).astype(jnp.bfloat16)
            up_term, down_term = after(up_term, *fence), after(down_term, *fence)
            travel[f] = both_ways(up_term, down_term, range(0, j))
            return list(travel[f])

        def weight_columns(f, other):
            lo, hi = bounds[f]
            pair = jnp.concatenate([down_weight[lo:hi], other], axis=1)
            return jnp.concatenate([pair, move(swap, pair, 1)], axis=1)

        def reduce_terms(f):
            dots = lax.dot_general(
                cot_rows, weights[f], KEEP_COLS, preferred_element_type=jnp.float32
            )
            return [dots[e * tokens : (e + 1) * tokens] for e in range(n_far)]

        def gathered_rows(f):
            slots = [after(hidden[f], *fence)]
            for e in range(1, n_far):
                above_e = after(above[f][e], *fence)
                below_e = after(below[f][n_far - e], *fence)
                slots.append(jnp.where(far + e < n_far, above_e, below_e))
            return jnp.concatenate(slots, axis=0)

        def grad_terms(f):
            give, keep = (
                lax.dot_general(rows[f], part, SUM_ROWS, preferred_element_type=jnp.float32)
                for part in (cot_rows[:, 2 * width :], cot_rows[:, : 2 * width])
            )
            theirs = swap(give.astype(jnp.bfloat16), 1)
            return (
                keep[:, :width] + theirs[:, :width].astype(jnp.float32),
                (keep[:, width:] + theirs[:, width:].astype(jnp.float32)).astype(jnp.bfloat16),
            )

        weights, terms, rows = {}, {}, {}

        parts = [cotangent] + [local_shift(cotangent, n_local - s) for s in range(1, n_local)]
        weight_side = swap(down_weight[:middle], 2)
        waits = gather_hop(0, 1)
        cot_slots = jnp.concatenate(parts, axis=1).reshape(tokens, n_far, QUAD, width)
        cot_slots = picked(cot_slots, [near ^ k for k in ORDER], 2).reshape(tokens, n_far, columns)

        def cot_for(step):
            place = (far + step) % n_far
            start = (place // per_half - x) % n_local * per_half + place % per_half
            return lax.dynamic_index_in_dim(cot_slots, start, axis=1, keepdims=False)

        came = []
        for e in range(1, n_far):
            came.append(shift(after(cot_for(n_far - e), *came[: max(0, e - 2)]), n_far - e))
        cot_rows = jnp.concatenate([cot_for(0)] + came, axis=0)
        fence = waits + came + [weight_side, hidden[1]]

        for j in range(2, n_far + 1):
            waits = []
            if j < n_far:
                waits += gather_hop(0, j)
            before = fence
            fence = fence + waits if j == 2 else fence
            waits += gather_hop(1, j - 1)
            fence = before
            if j == 2:
                weights[0] = weight_columns(0, weight_side)
                weight_side = move(swap, down_weight[middle:], 2)
                terms[0] = reduce_terms(0)
                waits.append(weight_side)
            waits += reduce_hop(0, j - 1)
            if j == 3:
                weights[1] = weight_columns(1, weight_side)
                terms[1] = reduce_terms(1)
            if j == n_far:
                rows[0] = gathered_rows(0)
                mine, give = grad_terms(0)
                grad_parts = [mine + swap(give, 2).astype(jnp.float32)]
                fence = fence + waits[:1] + [give]
                waits.append(give)
            if j > 2:
                waits += reduce_hop(1, j - 2)
            fence = waits

        waits = reduce_hop(1, last_hop)
        rows[1] = gathered_rows(1)
        mine, give = grad_terms(1)
        grad_parts.append(mine + swap(give, 2).astype(jnp.float32))
        out_sum = sum(
            jnp.dot(after(rows[f], *fence), weights[f], preferred_element_type=jnp.float32)
            for f in range(2)
        )
        out_terms = after(out_sum.astype(jnp.bfloat16), give, *waits)
        outs = [out_terms[:tokens]]
        for e in range(1, n_far):
            term = out_terms[e * tokens : (e + 1) * tokens]
            outs.append(shift(after(term, *outs[1 : max(1, e - 1)]), e))
        up_parts, gate_parts = [], []
        for f in range(2):
            up, down = travel[f]
            hidden_grad = terms[f][0] + up.astype(jnp.float32) + down.astype(jnp.float32)
            lo, hi = bounds[f]
            gate_wide = gate_act[:, lo:hi].astype(jnp.float32)
            up_wide = up_act[:, lo:hi].astype(jnp.float32)
            sigmoid_gate = jax.nn.sigmoid(gate_wide)
            up_parts.append((hidden_grad * gate_wide * sigmoid_gate).astype(jnp.bfloat16))
            gate_parts.append(
                (
                    hidden_grad * up_wide * sigmoid_gate * (1.0 + gate_wide * (1.0 - sigmoid_gate))
                ).astype(jnp.bfloat16)
            )

        out_slots = jnp.concatenate(outs, axis=1)

        def half_of(step):
            first = (x + step) % n_local * per_half
            starts = [(far - first - q) % n_far * columns for q in range(per_half)]
            return jnp.concatenate(
                [lax.dynamic_slice_in_dim(out_slots, s, columns, axis=1) for s in starts], axis=1
            )

        sides = [local_shift(half_of(step), step) for step in range(1, n_local)]
        output = half_of(0).astype(jnp.float32)
        for side in sides:
            output = output + side.astype(jnp.float32)
        output = output.astype(jnp.bfloat16).reshape(tokens, per_half, QUAD, width)
        return (
            picked(output, slot_of(near), 2).reshape(tokens, half),
            jnp.concatenate(gate_parts, axis=1),
            jnp.concatenate(up_parts, axis=1),
            jnp.concatenate(grad_parts, axis=0),
        )

    specs = (P("hst", "local"), P("hst", "local"), P("hst", "local"), P("local", "hst"))
    return jax.shard_map(
        on_device, mesh=mesh, in_specs=specs, out_specs=specs, check_vma=False
    )
```

```python
import jax
import jax.numpy as jnp
from jax import lax
from jax.sharding import PartitionSpec as P

QUAD = 4
ORDER = (0, 2, 1, 3)
KEEP_COLS = (((1,), (1,)), ((), ()))
SUM_ROWS = (((0,), (0,)), ((), ()))


def after(value, *others):
    return lax.optimization_barrier((value,) + others)[0] if others else value


def slot_of(near):
    return [((near ^ block) & 1) << 1 | (near ^ block) >> 1 for block in range(QUAD)]


def picked(view, places, axis):
    return jnp.concatenate(
        [lax.dynamic_slice_in_dim(view, place, 1, axis=axis) for place in places], axis=axis
    )


def solution(mesh):
    n_hst, n_local = mesh.shape["hst"], mesh.shape["local"]
    n_far = n_hst // QUAD
    last_hop = n_far - 1

    def swap(value, bit):
        return lax.ppermute(value, "hst", [(h, h ^ bit) for h in range(n_hst)])

    def shift(value, step):
        pairs = [(h, (h + step * QUAD) % n_hst) for h in range(n_hst)]
        return lax.ppermute(value, "hst", pairs)

    def far_permute(value, pairs):
        pairs = [(s * QUAD + q, t * QUAD + q) for s, t in pairs for q in range(QUAD)]
        return lax.ppermute(value, "hst", pairs)

    def both_ways(up, down, sources):
        return (
            far_permute(up, [(z, z + 1) for z in sources]),
            far_permute(down, [(n_far - 1 - z, n_far - 2 - z) for z in sources]),
        )

    def local_shift(value, step):
        return lax.ppermute(value, "local", [(i, (i + step) % n_local) for i in range(n_local)])

    def on_device(gate_act, up_act, cotangent, down_weight):
        h = lax.axis_index("hst")
        x = lax.axis_index("local")
        far, near = h // QUAD, h % QUAD
        tokens, half = cotangent.shape
        width = down_weight.shape[1]
        columns = QUAD * width
        hidden_units = gate_act.shape[1]
        per_half = half // columns
        middle = 128 * ((hidden_units // 128 + 1) // 2)
        bounds = [(0, middle), (middle, hidden_units)]

        fence = []

        def move(send, value, *args):
            return send(after(value, *fence), *args)

        gate_all, up_all = gate_act.astype(jnp.float32), up_act.astype(jnp.float32)
        hidden = (gate_all * jax.nn.sigmoid(gate_all) * up_all).astype(jnp.bfloat16)
        lower = far < n_far // 2

        above, below, travel = {}, {}, {}

        def gather_hop(j):
            up, down = (below[j - 1], above[j - 1]) if j > 1 else (hidden, hidden)
            if j == last_hop:
                one = after(jnp.where(lower, down, up), *fence)
                ends = [(n_far - 2, n_far - 1), (1, 0)]
                below[j] = above[j] = far_permute(one, ends)
                return [below[j]]
            up, down = after(up, *fence), after(down, *fence)
            below[j], above[j] = both_ways(up, down, range(j - 1, n_far - 1))
            return [below[j], above[j]]

        def reduce_hop(f, j):
            d = n_far - j
            up_term, down_term = terms[f][d], terms[f][n_far - d]
            if j == 1:
                one = after(jnp.where(lower, up_term, down_term), *fence)
                one = far_permute(one, [(0, 1), (n_far - 1, n_far - 2)])
                none = jnp.zeros_like(one)
                travel[f] = jnp.where(lower, one, none), jnp.where(lower, none, one)
                return [one]
            up, down = travel[f]
            up_term = (up_term.astype(jnp.float32) + up.astype(jnp.float32)).astype(jnp.bfloat16)
            down_term = down_term.astype(jnp.float32) + down.astype(jnp.float32)
            down_term = down_term.astype(jnp.bfloat16)
            up_term, down_term = after(up_term, *fence), after(down_term, *fence)
            travel[f] = both_ways(up_term, down_term, range(0, j))
            return list(travel[f])

        def weight_columns(f, other):
            lo, hi = bounds[f]
            pair = jnp.concatenate([down_weight[lo:hi], other], axis=1)
            return jnp.concatenate([pair, move(swap, pair, 1)], axis=1)

        def reduce_terms(f):
            dots = lax.dot_general(
                cot_rows, weights[f], KEEP_COLS, preferred_element_type=jnp.float32
            ).astype(jnp.bfloat16)
            return [dots[e * tokens : (e + 1) * tokens] for e in range(n_far)]

        weights, terms = {}, {}

        parts = [cotangent] + [local_shift(cotangent, n_local - s) for s in range(1, n_local)]
        weight_side = swap(down_weight[:middle], 2)
        waits = gather_hop(1)
        cot_slots = jnp.concatenate(parts, axis=1).reshape(tokens, n_far, QUAD, width)
        cot_slots = picked(cot_slots, [near ^ k for k in ORDER], 2).reshape(tokens, n_far, columns)

        def cot_for(step):
            place = (far + step) % n_far
            start = (place // per_half - x) % n_local * per_half + place % per_half
            return lax.dynamic_index_in_dim(cot_slots, start, axis=1, keepdims=False)

        came = []
        for e in range(1, n_far):
            came.append(shift(after(cot_for(n_far - e), *came[: max(0, e - 2)]), n_far - e))
        cot_rows = jnp.concatenate([cot_for(0)] + came, axis=0)
        fence = waits + came + [weight_side]

        for j in range(2, n_far):
            waits = gather_hop(j)
            if j == 2:
                weights[0] = weight_columns(0, weight_side)
                weight_side = move(swap, down_weight[middle:], 2)
                terms[0] = reduce_terms(0)
                waits.append(weight_side)
            waits += reduce_hop(0, j - 1)
            if j == 3:
                weights[1] = weight_columns(1, weight_side)
                terms[1] = reduce_terms(1)
            if j > 2:
                waits += reduce_hop(1, j - 2)
            fence = waits

        gather_fence, fence = fence, []
        waits = reduce_hop(0, last_hop)
        fence = gather_fence
        waits += reduce_hop(1, last_hop - 1)
        slots = [after(hidden, *fence)]
        for e in range(1, n_far):
            above_e, below_e = after(above[e], *fence), after(below[n_far - e], *fence)
            slots.append(jnp.where(far + e < n_far, above_e, below_e))
        rows = jnp.concatenate(slots, axis=0)

        def grad_terms(lo, hi):
            part = cot_rows[:, lo * width : hi * width]
            return lax.dot_general(rows, part, SUM_ROWS, preferred_element_type=jnp.float32)

        theirs = swap(grad_terms(2, 4).astype(jnp.bfloat16), 1)
        give = grad_terms(1, 2) + theirs[:, width:].astype(jnp.float32)
        give = give.astype(jnp.bfloat16)
        other_grad = swap(give, 2)
        for part in travel:
            travel[part] = tuple(after(value, give) for value in travel[part])
        rows = after(rows, give)
        down_grad = grad_terms(0, 1) + after(theirs, give)[:, :width].astype(jnp.float32)
        down_grad = down_grad + other_grad.astype(jnp.float32)
        out_sum = 0.0
        for f, (lo, hi) in enumerate(bounds):
            out_sum += jnp.dot(rows[:, lo:hi], weights[f], preferred_element_type=jnp.float32)
        out_terms = after(out_sum.astype(jnp.bfloat16), *waits)

        fence = waits + [give]
        waits = reduce_hop(1, last_hop)
        outs = [out_terms[:tokens]]
        for e in range(1, n_far):
            term = out_terms[e * tokens : (e + 1) * tokens]
            outs.append(shift(after(term, *outs[1 : max(1, e - 1)]), e))
        up_parts, gate_parts = [], []
        for f in range(2):
            up, down = travel[f]
            hidden_grad = terms[f][0].astype(jnp.float32) + up.astype(jnp.float32)
            hidden_grad += down.astype(jnp.float32)
            lo, hi = bounds[f]
            gate_wide = gate_act[:, lo:hi].astype(jnp.float32)
            up_wide = up_act[:, lo:hi].astype(jnp.float32)
            sigmoid_gate = jax.nn.sigmoid(gate_wide)
            up_parts.append((hidden_grad * gate_wide * sigmoid_gate).astype(jnp.bfloat16))
            gate_parts.append(
                (
                    hidden_grad * up_wide * sigmoid_gate * (1.0 + gate_wide * (1.0 - sigmoid_gate))
                ).astype(jnp.bfloat16)
            )

        out_slots = jnp.concatenate(outs, axis=1)

        def half_of(step):
            first = (x + step) % n_local * per_half
            starts = [(far - first - q) % n_far * columns for q in range(per_half)]
            return jnp.concatenate(
                [lax.dynamic_slice_in_dim(out_slots, s, columns, axis=1) for s in starts], axis=1
            )

        sides = [local_shift(half_of(step), step) for step in range(1, n_local)]
        output = half_of(0).astype(jnp.float32)
        for side in sides:
            output = output + after(side, down_grad).astype(jnp.float32)
        output = output.astype(jnp.bfloat16).reshape(tokens, per_half, QUAD, width)
        return (
            picked(output, slot_of(near), 2).reshape(tokens, half),
            jnp.concatenate(gate_parts, axis=1),
            jnp.concatenate(up_parts, axis=1),
            down_grad,
        )

    specs = (P("hst", "local"), P("hst", "local"), P("hst", "local"), P("local", "hst"))
    return jax.shard_map(
        on_device, mesh=mesh, in_specs=specs, out_specs=specs, check_vma=False
    )
```

```python
import jax
import jax.numpy as jnp
from jax import lax
from jax.sharding import PartitionSpec as P

QUAD = 4
ORDER = (0, 2, 1, 3)
KEEP_COLS = (((1,), (1,)), ((), ()))
SUM_ROWS = (((0,), (0,)), ((), ()))


def after(value, *others):
    return lax.optimization_barrier((value,) + others)[0] if others else value


def slot_of(near):
    return [((near ^ block) & 1) << 1 | (near ^ block) >> 1 for block in range(QUAD)]


def picked(view, places, axis):
    return jnp.concatenate(
        [lax.dynamic_slice_in_dim(view, place, 1, axis=axis) for place in places], axis=axis
    )


def solution(mesh):
    n_hst, n_local = mesh.shape["hst"], mesh.shape["local"]
    n_far = n_hst // QUAD
    last_hop = n_far - 1

    def swap(value, bit):
        return lax.ppermute(value, "hst", [(h, h ^ bit) for h in range(n_hst)])

    def shift(value, step):
        pairs = [(h, (h + step * QUAD) % n_hst) for h in range(n_hst)]
        return lax.ppermute(value, "hst", pairs)

    def far_permute(value, pairs):
        pairs = [(s * QUAD + q, t * QUAD + q) for s, t in pairs for q in range(QUAD)]
        return lax.ppermute(value, "hst", pairs)

    def both_ways(up, down, sources):
        return (
            far_permute(up, [(z, z + 1) for z in sources]),
            far_permute(down, [(n_far - 1 - z, n_far - 2 - z) for z in sources]),
        )

    def local_shift(value, step):
        return lax.ppermute(value, "local", [(i, (i + step) % n_local) for i in range(n_local)])

    def on_device(gate_act, up_act, cotangent, down_weight):
        h = lax.axis_index("hst")
        x = lax.axis_index("local")
        far, near = h // QUAD, h % QUAD
        tokens, half = cotangent.shape
        width = down_weight.shape[1]
        columns = QUAD * width
        hidden_units = gate_act.shape[1]
        per_half = half // columns
        middle = 128 * ((hidden_units // 128 + 1) // 2)
        bounds = [(0, middle), (middle, hidden_units)]

        fence = []

        def move(send, value, *args):
            return send(after(value, *fence), *args)

        gate_all, up_all = gate_act.astype(jnp.float32), up_act.astype(jnp.float32)
        hidden = (gate_all * jax.nn.sigmoid(gate_all) * up_all).astype(jnp.bfloat16)
        lower = far < n_far // 2

        above, below, travel = {}, {}, {}

        def gather_hop(j):
            up, down = (below[j - 1], above[j - 1]) if j > 1 else (hidden, hidden)
            if j == last_hop:
                one = after(jnp.where(lower, down, up), *fence)
                ends = [(n_far - 2, n_far - 1), (1, 0)]
                below[j] = above[j] = far_permute(one, ends)
                return [below[j]]
            up, down = after(up, *fence), after(down, *fence)
            below[j], above[j] = both_ways(up, down, range(j - 1, n_far - 1))
            return [below[j], above[j]]

        def reduce_hop(f, j):
            d = n_far - j
            up_term, down_term = terms[f][d], terms[f][n_far - d]
            if j == 1:
                one = after(jnp.where(lower, up_term, down_term), *fence)
                one = far_permute(one, [(0, 1), (n_far - 1, n_far - 2)])
                none = jnp.zeros_like(one)
                travel[f] = jnp.where(lower, one, none), jnp.where(lower, none, one)
                return [one]
            up, down = travel[f]
            up_term = (up_term.astype(jnp.float32) + up.astype(jnp.float32)).astype(jnp.bfloat16)
            down_term = down_term.astype(jnp.float32) + down.astype(jnp.float32)
            down_term = down_term.astype(jnp.bfloat16)
            up_term, down_term = after(up_term, *fence), after(down_term, *fence)
            travel[f] = both_ways(up_term, down_term, range(0, j))
            return list(travel[f])

        def weight_columns(f, other):
            lo, hi = bounds[f]
            pair = jnp.concatenate([down_weight[lo:hi], other], axis=1)
            far_pairs[f] = move(swap, pair, 1)
            return jnp.concatenate([pair, far_pairs[f]], axis=1)

        def reduce_terms(f):
            dots = lax.dot_general(
                cot_rows, weights[f], KEEP_COLS, preferred_element_type=jnp.float32
            ).astype(jnp.bfloat16)
            return [dots[e * tokens : (e + 1) * tokens] for e in range(n_far)]

        weights, far_pairs, terms = {}, {}, {}

        parts = [cotangent] + [local_shift(cotangent, n_local - s) for s in range(1, n_local)]
        weight_side = swap(after(down_weight[:middle], hidden), 2)
        waits = gather_hop(1)
        cot_slots = jnp.concatenate(parts, axis=1).reshape(tokens, n_far, QUAD, width)
        cot_slots = picked(cot_slots, [near ^ k for k in ORDER], 2).reshape(tokens, n_far, columns)

        def cot_for(step):
            place = (far + step) % n_far
            start = (place // per_half - x) % n_local * per_half + place % per_half
            return lax.dynamic_index_in_dim(cot_slots, start, axis=1, keepdims=False)

        came = []
        for e in range(1, n_far):
            came.append(shift(after(cot_for(n_far - e), *came[: max(0, e - 2)]), n_far - e))
        cot_rows = jnp.concatenate([cot_for(0)] + came, axis=0)
        fence = waits + came + [weight_side]

        for j in range(2, n_far):
            waits = gather_hop(j)
            if j == 2:
                weights[0] = weight_columns(0, weight_side)
                weight_side = move(swap, down_weight[middle:], 2)
                terms[0] = reduce_terms(0)
                waits.append(weight_side)
            if j == 3:
                weights[1] = weight_columns(1, weight_side)
                terms[1] = reduce_terms(1)
                fence = fence + [far_pairs[1]]
            waits += reduce_hop(0, j - 1)
            if j > 2:
                waits += reduce_hop(1, j - 2)
            fence = waits

        gather_fence, fence = fence, []
        waits = reduce_hop(0, last_hop)
        fence = gather_fence
        waits += reduce_hop(1, last_hop - 1)
        slots = [after(hidden, *fence)]
        for e in range(1, n_far):
            above_e, below_e = after(above[e], *fence), after(below[n_far - e], *fence)
            slots.append(jnp.where(far + e < n_far, above_e, below_e))
        rows = jnp.concatenate(slots, axis=0)

        def grad_terms(lo, hi):
            part = cot_rows[:, lo * width : hi * width]
            return lax.dot_general(rows, part, SUM_ROWS, preferred_element_type=jnp.float32)

        theirs = swap(grad_terms(2, 4).astype(jnp.bfloat16), 1)
        give = grad_terms(1, 2) + theirs[:, width:].astype(jnp.float32)
        give = give.astype(jnp.bfloat16)
        other_grad = swap(give, 2)
        rows = after(rows, give)
        down_grad = grad_terms(0, 1) + after(theirs, give)[:, :width].astype(jnp.float32)
        down_grad = down_grad + other_grad.astype(jnp.float32)
        out_sum = 0.0
        for f, (lo, hi) in enumerate(bounds):
            out_sum += jnp.dot(rows[:, lo:hi], weights[f], preferred_element_type=jnp.float32)
            if f == 0:
                for part in travel:
                    travel[part] = tuple(after(value, out_sum) for value in travel[part])
        out_terms = after(out_sum.astype(jnp.bfloat16), *waits)

        fence = waits + [give, out_terms]
        waits = reduce_hop(1, last_hop)
        outs = [out_terms[:tokens]]
        for e in range(1, n_far):
            term = out_terms[e * tokens : (e + 1) * tokens]
            outs.append(shift(after(term, *outs[1 : max(1, e - 1)]), e))
        up_parts, gate_parts = [], []
        for f in range(2):
            up, down = travel[f]
            hidden_grad = terms[f][0].astype(jnp.float32) + up.astype(jnp.float32)
            hidden_grad += down.astype(jnp.float32)
            lo, hi = bounds[f]
            gate_wide = gate_act[:, lo:hi].astype(jnp.float32)
            up_wide = up_act[:, lo:hi].astype(jnp.float32)
            sigmoid_gate = jax.nn.sigmoid(gate_wide)
            up_parts.append((hidden_grad * gate_wide * sigmoid_gate).astype(jnp.bfloat16))
            gate_parts.append(
                (
                    hidden_grad * up_wide * sigmoid_gate * (1.0 + gate_wide * (1.0 - sigmoid_gate))
                ).astype(jnp.bfloat16)
            )

        out_slots = jnp.concatenate(outs, axis=1)

        def half_of(step):
            first = (x + step) % n_local * per_half
            starts = [(far - first - q) % n_far * columns for q in range(per_half)]
            return jnp.concatenate(
                [lax.dynamic_slice_in_dim(out_slots, s, columns, axis=1) for s in starts], axis=1
            )

        sides = [local_shift(half_of(step), step) for step in range(1, n_local)]
        output = half_of(0).astype(jnp.float32)
        for side in sides:
            output = output + after(side, down_grad).astype(jnp.float32)
        output = output.astype(jnp.bfloat16).reshape(tokens, per_half, QUAD, width)
        return (
            picked(output, slot_of(near), 2).reshape(tokens, half),
            jnp.concatenate(gate_parts, axis=1),
            jnp.concatenate(up_parts, axis=1),
            down_grad,
        )

    specs = (P("hst", "local"), P("hst", "local"), P("hst", "local"), P("local", "hst"))
    return jax.shard_map(
        on_device, mesh=mesh, in_specs=specs, out_specs=specs, check_vma=False
    )
```

```python
import jax
import jax.numpy as jnp
from jax import lax
from jax.sharding import PartitionSpec as P

QUAD = 4
ORDER = (0, 2, 1, 3)
KEEP_COLS = (((1,), (1,)), ((), ()))
SUM_ROWS = (((0,), (0,)), ((), ()))


def after(value, *others):
    return lax.optimization_barrier((value,) + others)[0] if others else value


def slot_of(near):
    return [((near ^ block) & 1) << 1 | (near ^ block) >> 1 for block in range(QUAD)]


def picked(view, places, axis):
    return jnp.concatenate(
        [lax.dynamic_slice_in_dim(view, place, 1, axis=axis) for place in places], axis=axis
    )


def solution(mesh):
    n_hst, n_local = mesh.shape["hst"], mesh.shape["local"]
    n_far = n_hst // QUAD
    last_hop = n_far - 1

    def swap(value, bit):
        return lax.ppermute(value, "hst", [(h, h ^ bit) for h in range(n_hst)])

    def shift(value, step):
        pairs = [(h, (h + step * QUAD) % n_hst) for h in range(n_hst)]
        return lax.ppermute(value, "hst", pairs)

    def far_permute(value, pairs):
        pairs = [(s * QUAD + q, t * QUAD + q) for s, t in pairs for q in range(QUAD)]
        return lax.ppermute(value, "hst", pairs)

    def both_ways(up, down, sources):
        return (
            far_permute(up, [(z, z + 1) for z in sources]),
            far_permute(down, [(n_far - 1 - z, n_far - 2 - z) for z in sources]),
        )

    def local_shift(value, step):
        return lax.ppermute(value, "local", [(i, (i + step) % n_local) for i in range(n_local)])

    def on_device(gate_act, up_act, cotangent, down_weight):
        h = lax.axis_index("hst")
        x = lax.axis_index("local")
        far, near = h // QUAD, h % QUAD
        tokens, half = cotangent.shape
        width = down_weight.shape[1]
        columns = QUAD * width
        hidden_units = gate_act.shape[1]
        per_half = half // columns
        middle = 128 * ((hidden_units // 128 + 1) // 2)
        bounds = [(0, middle), (middle, hidden_units)]

        fence = []

        def move(send, value, *args):
            return send(after(value, *fence), *args)

        gate_all, up_all = gate_act.astype(jnp.float32), up_act.astype(jnp.float32)
        hidden = (gate_all * jax.nn.sigmoid(gate_all) * up_all).astype(jnp.bfloat16)
        lower = far < n_far // 2

        above, below, travel = {}, {}, {}

        def gather_hop(j):
            up, down = (below[j - 1], above[j - 1]) if j > 1 else (hidden, hidden)
            if j == last_hop:
                one = after(jnp.where(lower, down, up), *fence)
                ends = [(n_far - 2, n_far - 1), (1, 0)]
                below[j] = above[j] = far_permute(one, ends)
                return [below[j]]
            up, down = after(up, *fence), after(down, *fence)
            below[j], above[j] = both_ways(up, down, range(j - 1, n_far - 1))
            return [below[j], above[j]]

        def reduce_hop(f, j):
            d = n_far - j
            up_term, down_term = terms[f][d], terms[f][n_far - d]
            if j == 1:
                one = after(jnp.where(lower, up_term, down_term), *fence)
                one = far_permute(one, [(0, 1), (n_far - 1, n_far - 2)])
                none = jnp.zeros_like(one)
                travel[f] = jnp.where(lower, one, none), jnp.where(lower, none, one)
                return [one]
            up, down = travel[f]
            up_term = (up_term.astype(jnp.float32) + up.astype(jnp.float32)).astype(jnp.bfloat16)
            down_term = down_term.astype(jnp.float32) + down.astype(jnp.float32)
            down_term = down_term.astype(jnp.bfloat16)
            up_term, down_term = after(up_term, *fence), after(down_term, *fence)
            travel[f] = both_ways(up_term, down_term, range(0, j))
            return list(travel[f])

        def weight_columns(f, other):
            lo, hi = bounds[f]
            pair = jnp.concatenate([down_weight[lo:hi], other], axis=1)
            far_pairs[f] = move(swap, pair, 1)
            return jnp.concatenate([pair, far_pairs[f]], axis=1)

        def reduce_terms(f):
            dots = lax.dot_general(
                cot_rows, weights[f], KEEP_COLS, preferred_element_type=jnp.float32
            ).astype(jnp.bfloat16)
            return [dots[e * tokens : (e + 1) * tokens] for e in range(n_far)]

        weights, far_pairs, terms = {}, {}, {}

        parts = [cotangent] + [local_shift(cotangent, n_local - s) for s in range(1, n_local)]
        weight_side = swap(after(down_weight[:middle], hidden), 2)
        waits = gather_hop(1)
        cot_slots = jnp.concatenate(parts, axis=1).reshape(tokens, n_far, QUAD, width)
        cot_slots = picked(cot_slots, [near ^ k for k in ORDER], 2).reshape(tokens, n_far, columns)

        def cot_for(step):
            place = (far + step) % n_far
            start = (place // per_half - x) % n_local * per_half + place % per_half
            return lax.dynamic_index_in_dim(cot_slots, start, axis=1, keepdims=False)

        came = []
        for e in range(1, n_far):
            came.append(shift(after(cot_for(n_far - e), *came[: max(0, e - 2)]), n_far - e))
        cot_rows = jnp.concatenate([cot_for(0)] + came, axis=0)
        fence = waits + came + [weight_side]

        for j in range(2, n_far):
            waits = gather_hop(j)
            if j == 2:
                weights[0] = weight_columns(0, weight_side)
                weight_side = move(swap, down_weight[middle:], 2)
                terms[0] = reduce_terms(0)
                waits.append(weight_side)
            if j == 3:
                weights[1] = weight_columns(1, weight_side)
                terms[1] = reduce_terms(1)
                fence = fence + [far_pairs[1]]
            waits += reduce_hop(0, j - 1)
            if j > 2:
                waits += reduce_hop(1, j - 2)
            fence = waits

        gather_fence, fence = fence, []
        waits = reduce_hop(0, last_hop)
        fence = gather_fence
        waits += reduce_hop(1, last_hop - 1)
        slots = [after(hidden, *fence)]
        for e in range(1, n_far):
            above_e, below_e = after(above[e], *fence), after(below[n_far - e], *fence)
            slots.append(jnp.where(far + e < n_far, above_e, below_e))
        rows = jnp.concatenate(slots, axis=0)

        def grad_terms(lo, hi):
            part = cot_rows[:, lo * width : hi * width]
            return lax.dot_general(rows, part, SUM_ROWS, preferred_element_type=jnp.float32)

        theirs = swap(after(grad_terms(2, 4).astype(jnp.bfloat16), *travel[0]), 1)
        give = grad_terms(1, 2) + theirs[:, width:].astype(jnp.float32)
        give = give.astype(jnp.bfloat16)
        other_grad = swap(give, 2)
        rows = after(rows, give)
        down_grad = grad_terms(0, 1) + after(theirs, give)[:, :width].astype(jnp.float32)
        down_grad = down_grad + other_grad.astype(jnp.float32)
        out_sum = 0.0
        for f, (lo, hi) in enumerate(bounds):
            out_sum += jnp.dot(rows[:, lo:hi], weights[f], preferred_element_type=jnp.float32)
            if f == 0:
                for part in travel:
                    travel[part] = tuple(after(value, out_sum) for value in travel[part])
        out_terms = after(out_sum.astype(jnp.bfloat16), *waits)

        fence = waits + [give, out_terms]
        waits = reduce_hop(1, last_hop)
        outs = [out_terms[:tokens]]
        for e in range(1, n_far):
            term = out_terms[e * tokens : (e + 1) * tokens]
            outs.append(shift(after(term, *outs[1 : max(1, e - 1)]), e))
        up_parts, gate_parts = [], []
        for f in range(2):
            up, down = travel[f]
            hidden_grad = terms[f][0].astype(jnp.float32) + up.astype(jnp.float32)
            hidden_grad += down.astype(jnp.float32)
            lo, hi = bounds[f]
            gate_wide = gate_act[:, lo:hi].astype(jnp.float32)
            up_wide = up_act[:, lo:hi].astype(jnp.float32)
            sigmoid_gate = jax.nn.sigmoid(gate_wide)
            up_parts.append((hidden_grad * gate_wide * sigmoid_gate).astype(jnp.bfloat16))
            gate_parts.append(
                (
                    hidden_grad * up_wide * sigmoid_gate * (1.0 + gate_wide * (1.0 - sigmoid_gate))
                ).astype(jnp.bfloat16)
            )

        out_slots = jnp.concatenate(outs, axis=1)

        def half_of(step):
            first = (x + step) % n_local * per_half
            starts = [(far - first - q) % n_far * columns for q in range(per_half)]
            return jnp.concatenate(
                [lax.dynamic_slice_in_dim(out_slots, s, columns, axis=1) for s in starts], axis=1
            )

        sides = [local_shift(half_of(step), step) for step in range(1, n_local)]
        output = half_of(0).astype(jnp.float32)
        for side in sides:
            output = output + after(side, down_grad).astype(jnp.float32)
        output = output.astype(jnp.bfloat16).reshape(tokens, per_half, QUAD, width)
        return (
            picked(output, slot_of(near), 2).reshape(tokens, half),
            jnp.concatenate(gate_parts, axis=1),
            jnp.concatenate(up_parts, axis=1),
            down_grad,
        )

    specs = (P("hst", "local"), P("hst", "local"), P("hst", "local"), P("local", "hst"))
    return jax.shard_map(
        on_device, mesh=mesh, in_specs=specs, out_specs=specs, check_vma=False
    )
```

```python
import jax
import jax.numpy as jnp
from jax import lax
from jax.sharding import PartitionSpec as P

QUAD = 4
ORDER = (0, 2, 1, 3)
KEEP_COLS = (((1,), (1,)), ((), ()))
SUM_ROWS = (((0,), (0,)), ((), ()))


def after(value, *others):
    return lax.optimization_barrier((value,) + others)[0] if others else value


def slot_of(near):
    return [((near ^ block) & 1) << 1 | (near ^ block) >> 1 for block in range(QUAD)]


def picked(view, places, axis):
    return jnp.concatenate(
        [lax.dynamic_slice_in_dim(view, place, 1, axis=axis) for place in places], axis=axis
    )


def solution(mesh):
    n_hst, n_local = mesh.shape["hst"], mesh.shape["local"]
    n_far = n_hst // QUAD
    last_hop = n_far - 1

    def swap(value, bit):
        return lax.ppermute(value, "hst", [(h, h ^ bit) for h in range(n_hst)])

    def shift(value, step):
        pairs = [(h, (h + step * QUAD) % n_hst) for h in range(n_hst)]
        return lax.ppermute(value, "hst", pairs)

    def far_permute(value, pairs):
        pairs = [(s * QUAD + q, t * QUAD + q) for s, t in pairs for q in range(QUAD)]
        return lax.ppermute(value, "hst", pairs)

    def both_ways(up, down, sources):
        return (
            far_permute(up, [(z, z + 1) for z in sources]),
            far_permute(down, [(n_far - 1 - z, n_far - 2 - z) for z in sources]),
        )

    def local_shift(value, step):
        return lax.ppermute(value, "local", [(i, (i + step) % n_local) for i in range(n_local)])

    def on_device(gate_act, up_act, cotangent, down_weight):
        h = lax.axis_index("hst")
        x = lax.axis_index("local")
        far, near = h // QUAD, h % QUAD
        tokens, half = cotangent.shape
        width = down_weight.shape[1]
        columns = QUAD * width
        hidden_units = gate_act.shape[1]
        per_half = half // columns
        middle = 128 * ((hidden_units // 128 + 1) // 2)
        bounds = [(0, middle), (middle, hidden_units)]

        fence = []

        def move(send, value, *args):
            return send(after(value, *fence), *args)

        gate_all, up_all = gate_act.astype(jnp.float32), up_act.astype(jnp.float32)
        hidden = (gate_all * jax.nn.sigmoid(gate_all) * up_all).astype(jnp.bfloat16)
        lower = far < n_far // 2

        above, below, travel = {}, {}, {}

        def gather_hop(j):
            up, down = (below[j - 1], above[j - 1]) if j > 1 else (hidden, hidden)
            if j == last_hop:
                one = after(jnp.where(lower, down, up), *fence)
                ends = [(n_far - 2, n_far - 1), (1, 0)]
                below[j] = above[j] = far_permute(one, ends)
                return [below[j]]
            up, down = after(up, *fence), after(down, *fence)
            below[j], above[j] = both_ways(up, down, range(j - 1, n_far - 1))
            return [below[j], above[j]]

        def reduce_hop(f, j):
            d = n_far - j
            up_term, down_term = terms[f][d], terms[f][n_far - d]
            if j == 1:
                one = after(jnp.where(lower, up_term, down_term), *fence)
                one = far_permute(one, [(0, 1), (n_far - 1, n_far - 2)])
                none = jnp.zeros_like(one)
                travel[f] = jnp.where(lower, one, none), jnp.where(lower, none, one)
                return [one]
            up, down = travel[f]
            up_term = (up_term.astype(jnp.float32) + up.astype(jnp.float32)).astype(jnp.bfloat16)
            down_term = down_term.astype(jnp.float32) + down.astype(jnp.float32)
            down_term = down_term.astype(jnp.bfloat16)
            up_term, down_term = after(up_term, *fence), after(down_term, *fence)
            travel[f] = both_ways(up_term, down_term, range(0, j))
            return list(travel[f])

        def weight_columns(f, other):
            lo, hi = bounds[f]
            pair = jnp.concatenate([down_weight[lo:hi], other], axis=1)
            far_pairs[f] = move(swap, pair, 1)
            return jnp.concatenate([pair, far_pairs[f]], axis=1)

        def reduce_terms(f):
            dots = lax.dot_general(
                cot_rows, weights[f], KEEP_COLS, preferred_element_type=jnp.float32
            ).astype(jnp.bfloat16)
            return [dots[e * tokens : (e + 1) * tokens] for e in range(n_far)]

        weights, far_pairs, terms = {}, {}, {}

        parts = [cotangent] + [local_shift(cotangent, n_local - s) for s in range(1, n_local)]
        weight_side = swap(after(down_weight[:middle], hidden), 2)
        waits = gather_hop(1)
        cot_slots = jnp.concatenate(parts, axis=1).reshape(tokens, n_far, QUAD, width)
        cot_slots = picked(cot_slots, [near ^ k for k in ORDER], 2).reshape(tokens, n_far, columns)

        block = tokens // n_local

        def cot_for(step, first_row, count):
            place = (far + step) % n_far
            start = (place // per_half - x) % n_local * per_half + place % per_half
            found = lax.dynamic_slice(cot_slots, (first_row, start, 0), (count, 1, columns))
            return found.reshape(count, columns)

        came = []
        for e in range(1, n_far):
            sent = cot_for(n_far - e, x * block, block)
            came.append(shift(after(sent, *came[: max(0, e - 2)]), n_far - e))
        fence = waits + came + [weight_side]

        def whole_rows():
            mine = jnp.concatenate(came, axis=0)
            sides = [mine] + [move(local_shift, mine, n_local - i) for i in range(1, n_local)]
            blocks = []
            for i in range(n_local):
                picked_block = sides[0]
                for turn in range(1, n_local):
                    here = (i - x) % n_local == turn
                    picked_block = jnp.where(here, sides[turn], picked_block)
                blocks.append(picked_block.reshape(n_far - 1, block, columns))
            others = jnp.concatenate(blocks, axis=1).reshape((n_far - 1) * tokens, columns)
            return jnp.concatenate([cot_for(0, 0, tokens), others], axis=0)

        for j in range(2, n_far):
            waits = gather_hop(j)
            if j == 2:
                cot_rows = whole_rows()
                weights[0] = weight_columns(0, weight_side)
                weight_side = move(swap, down_weight[middle:], 2)
                terms[0] = reduce_terms(0)
                waits.append(weight_side)
            if j == 3:
                weights[1] = weight_columns(1, weight_side)
                terms[1] = reduce_terms(1)
                fence = fence + [far_pairs[1]]
            waits += reduce_hop(0, j - 1)
            if j > 2:
                waits += reduce_hop(1, j - 2)
            fence = waits

        gather_fence, fence = fence, []
        waits = reduce_hop(0, last_hop)
        fence = gather_fence
        waits += reduce_hop(1, last_hop - 1)
        slots = [after(hidden, *fence)]
        for e in range(1, n_far):
            above_e, below_e = after(above[e], *fence), after(below[n_far - e], *fence)
            slots.append(jnp.where(far + e < n_far, above_e, below_e))
        rows = jnp.concatenate(slots, axis=0)

        def grad_terms(lo, hi):
            part = cot_rows[:, lo * width : hi * width]
            return lax.dot_general(rows, part, SUM_ROWS, preferred_element_type=jnp.float32)

        theirs = swap(after(grad_terms(2, 4).astype(jnp.bfloat16), *travel[0]), 1)
        give = grad_terms(1, 2) + theirs[:, width:].astype(jnp.float32)
        give = give.astype(jnp.bfloat16)
        other_grad = swap(give, 2)
        rows = after(rows, give)
        down_grad = grad_terms(0, 1) + after(theirs, give)[:, :width].astype(jnp.float32)
        down_grad = down_grad + other_grad.astype(jnp.float32)
        out_sum = 0.0
        for f, (lo, hi) in enumerate(bounds):
            out_sum += jnp.dot(rows[:, lo:hi], weights[f], preferred_element_type=jnp.float32)
            if f == 0:
                for part in travel:
                    travel[part] = tuple(after(value, out_sum) for value in travel[part])
        out_terms = after(out_sum.astype(jnp.bfloat16), *waits)

        fence = waits + [give, out_terms]
        waits = reduce_hop(1, last_hop)
        outs = [out_terms[:tokens]]
        for e in range(1, n_far):
            term = out_terms[e * tokens : (e + 1) * tokens]
            outs.append(shift(after(term, *outs[1 : max(1, e - 1)]), e))
        up_parts, gate_parts = [], []
        for f in range(2):
            up, down = travel[f]
            hidden_grad = terms[f][0].astype(jnp.float32) + up.astype(jnp.float32)
            hidden_grad += down.astype(jnp.float32)
            lo, hi = bounds[f]
            gate_wide = gate_act[:, lo:hi].astype(jnp.float32)
            up_wide = up_act[:, lo:hi].astype(jnp.float32)
            sigmoid_gate = jax.nn.sigmoid(gate_wide)
            up_parts.append((hidden_grad * gate_wide * sigmoid_gate).astype(jnp.bfloat16))
            gate_parts.append(
                (
                    hidden_grad * up_wide * sigmoid_gate * (1.0 + gate_wide * (1.0 - sigmoid_gate))
                ).astype(jnp.bfloat16)
            )

        out_slots = jnp.concatenate(outs, axis=1)

        def half_of(step):
            first = (x + step) % n_local * per_half
            starts = [(far - first - q) % n_far * columns for q in range(per_half)]
            return jnp.concatenate(
                [lax.dynamic_slice_in_dim(out_slots, s, columns, axis=1) for s in starts], axis=1
            )

        sides = [local_shift(half_of(step), step) for step in range(1, n_local)]
        output = half_of(0).astype(jnp.float32)
        for side in sides:
            output = output + after(side, down_grad).astype(jnp.float32)
        output = output.astype(jnp.bfloat16).reshape(tokens, per_half, QUAD, width)
        return (
            picked(output, slot_of(near), 2).reshape(tokens, half),
            jnp.concatenate(gate_parts, axis=1),
            jnp.concatenate(up_parts, axis=1),
            down_grad,
        )

    specs = (P("hst", "local"), P("hst", "local"), P("hst", "local"), P("local", "hst"))
    return jax.shard_map(
        on_device, mesh=mesh, in_specs=specs, out_specs=specs, check_vma=False
    )
```

```python
import jax
import jax.numpy as jnp
from jax import lax
from jax.sharding import PartitionSpec as P

QUAD = 4
ORDER = (0, 2, 1, 3)
KEEP_COLS = (((1,), (1,)), ((), ()))
SUM_ROWS = (((0,), (0,)), ((), ()))


def after(value, *others):
    return lax.optimization_barrier((value,) + others)[0] if others else value


def slot_of(near):
    return [((near ^ block) & 1) << 1 | (near ^ block) >> 1 for block in range(QUAD)]


def picked(view, places, axis):
    return jnp.concatenate(
        [lax.dynamic_slice_in_dim(view, place, 1, axis=axis) for place in places], axis=axis
    )


def solution(mesh):
    n_hst, n_local = mesh.shape["hst"], mesh.shape["local"]
    n_far = n_hst // QUAD
    last_hop = n_far - 1

    def swap(value, bit):
        return lax.ppermute(value, "hst", [(h, h ^ bit) for h in range(n_hst)])

    def shift(value, step):
        pairs = [(h, (h + step * QUAD) % n_hst) for h in range(n_hst)]
        return lax.ppermute(value, "hst", pairs)

    def far_permute(value, pairs):
        pairs = [(s * QUAD + q, t * QUAD + q) for s, t in pairs for q in range(QUAD)]
        return lax.ppermute(value, "hst", pairs)

    def both_ways(up, down, sources):
        return (
            far_permute(up, [(z, z + 1) for z in sources]),
            far_permute(down, [(n_far - 1 - z, n_far - 2 - z) for z in sources]),
        )

    def local_shift(value, step):
        return lax.ppermute(value, "local", [(i, (i + step) % n_local) for i in range(n_local)])

    def on_device(gate_act, up_act, cotangent, down_weight):
        h = lax.axis_index("hst")
        x = lax.axis_index("local")
        far, near = h // QUAD, h % QUAD
        tokens, half = cotangent.shape
        width = down_weight.shape[1]
        columns = QUAD * width
        hidden_units = gate_act.shape[1]
        per_half = half // columns
        middle = 128 * ((hidden_units // 128 + 1) // 2)
        bounds = [(0, middle), (middle, hidden_units)]

        fence = []

        def move(send, value, *args):
            return send(after(value, *fence), *args)

        gate_all, up_all = gate_act.astype(jnp.float32), up_act.astype(jnp.float32)
        hidden = (gate_all * jax.nn.sigmoid(gate_all) * up_all).astype(jnp.bfloat16)
        lower = far < n_far // 2

        above, below, travel = {}, {}, {}

        def gather_hop(j):
            up, down = (below[j - 1], above[j - 1]) if j > 1 else (hidden, hidden)
            if j == last_hop:
                one = after(jnp.where(lower, down, up), *fence)
                ends = [(n_far - 2, n_far - 1), (1, 0)]
                below[j] = above[j] = far_permute(one, ends)
                return [below[j]]
            up, down = after(up, *fence), after(down, *fence)
            below[j], above[j] = both_ways(up, down, range(j - 1, n_far - 1))
            return [below[j], above[j]]

        def reduce_hop(f, j):
            d = n_far - j
            up_term, down_term = terms[f][d], terms[f][n_far - d]
            if j == 1:
                one = after(jnp.where(lower, up_term, down_term), *fence)
                one = far_permute(one, [(0, 1), (n_far - 1, n_far - 2)])
                none = jnp.zeros_like(one)
                travel[f] = jnp.where(lower, one, none), jnp.where(lower, none, one)
                return [one]
            up, down = travel[f]
            up_term = (up_term.astype(jnp.float32) + up.astype(jnp.float32)).astype(jnp.bfloat16)
            down_term = down_term.astype(jnp.float32) + down.astype(jnp.float32)
            down_term = down_term.astype(jnp.bfloat16)
            up_term, down_term = after(up_term, *fence), after(down_term, *fence)
            travel[f] = both_ways(up_term, down_term, range(0, j))
            return list(travel[f])

        def weight_columns(f, other):
            lo, hi = bounds[f]
            pair = jnp.concatenate([down_weight[lo:hi], other], axis=1)
            far_pairs[f] = move(swap, pair, 1)
            return jnp.concatenate([pair, far_pairs[f]], axis=1)

        def reduce_terms(f):
            dots = lax.dot_general(
                cot_rows, weights[f], KEEP_COLS, preferred_element_type=jnp.float32
            ).astype(jnp.bfloat16)
            return [dots[e * tokens : (e + 1) * tokens] for e in range(n_far)]

        weights, far_pairs, terms = {}, {}, {}

        parts = [cotangent] + [local_shift(cotangent, n_local - s) for s in range(1, n_local)]
        weight_side = swap(after(down_weight[:middle], hidden), 2)
        waits = gather_hop(1)
        cot_slots = jnp.concatenate(parts, axis=1).reshape(tokens, n_far, QUAD, width)
        cot_slots = picked(cot_slots, [near ^ k for k in ORDER], 2).reshape(tokens, n_far, columns)

        block = tokens // n_local

        def cot_for(step, first_row, count):
            place = (far + step) % n_far
            start = (place // per_half - x) % n_local * per_half + place % per_half
            found = lax.dynamic_slice(cot_slots, (first_row, start, 0), (count, 1, columns))
            return found.reshape(count, columns)

        came = []
        for e in range(1, n_far):
            sent = cot_for(n_far - e, x * block, block)
            came.append(shift(after(sent, *came[: max(0, e - 2)]), n_far - e))
        second_weight = lax.optimization_barrier(down_weight[middle:])
        fence = waits + came + [weight_side, second_weight]

        def whole_rows():
            mine = jnp.concatenate(came, axis=0)
            sides = [mine] + [move(local_shift, mine, n_local - i) for i in range(1, n_local)]
            blocks = []
            for i in range(n_local):
                picked_block = sides[0]
                for turn in range(1, n_local):
                    here = (i - x) % n_local == turn
                    picked_block = jnp.where(here, sides[turn], picked_block)
                blocks.append(picked_block.reshape(n_far - 1, block, columns))
            others = jnp.concatenate(blocks, axis=1).reshape((n_far - 1) * tokens, columns)
            return jnp.concatenate([cot_for(0, 0, tokens), others], axis=0)

        for j in range(2, n_far):
            waits = gather_hop(j)
            if j == 2:
                cot_rows = whole_rows()
                weights[0] = weight_columns(0, weight_side)
                weight_side = move(swap, second_weight, 2)
                terms[0] = reduce_terms(0)
                waits.append(weight_side)
            if j == 3:
                weights[1] = weight_columns(1, weight_side)
                terms[1] = reduce_terms(1)
                fence = fence + [far_pairs[1]]
            waits += reduce_hop(0, j - 1)
            if j > 2:
                waits += reduce_hop(1, j - 2)
            fence = waits

        gather_fence, fence = fence, []
        waits = reduce_hop(0, last_hop)
        fence = gather_fence
        waits += reduce_hop(1, last_hop - 1)
        slots = [after(hidden, *fence)]
        for e in range(1, n_far):
            above_e, below_e = after(above[e], *fence), after(below[n_far - e], *fence)
            slots.append(jnp.where(far + e < n_far, above_e, below_e))
        rows = jnp.concatenate(slots, axis=0)

        def grad_terms(lo, hi):
            part = cot_rows[:, lo * width : hi * width]
            return lax.dot_general(rows, part, SUM_ROWS, preferred_element_type=jnp.float32)

        theirs = swap(after(grad_terms(2, 4).astype(jnp.bfloat16), *travel[0]), 1)
        give = grad_terms(1, 2) + theirs[:, width:].astype(jnp.float32)
        give = give.astype(jnp.bfloat16)
        other_grad = swap(give, 2)
        rows = after(rows, give)
        down_grad = grad_terms(0, 1) + after(theirs, give)[:, :width].astype(jnp.float32)
        down_grad = down_grad + other_grad.astype(jnp.float32)
        out_sum = 0.0
        for f, (lo, hi) in enumerate(bounds):
            out_sum += jnp.dot(rows[:, lo:hi], weights[f], preferred_element_type=jnp.float32)
            if f == 0:
                for part in travel:
                    travel[part] = tuple(after(value, out_sum) for value in travel[part])
        out_terms = after(out_sum.astype(jnp.bfloat16), *waits)

        fence = waits + [give, out_terms]
        waits = reduce_hop(1, last_hop)
        outs = [out_terms[:tokens]]
        for e in range(1, n_far):
            term = out_terms[e * tokens : (e + 1) * tokens]
            outs.append(shift(after(term, *outs[1 : max(1, e - 1)]), e))
        up_parts, gate_parts = [], []
        for f in range(2):
            up, down = travel[f]
            hidden_grad = terms[f][0].astype(jnp.float32) + up.astype(jnp.float32)
            hidden_grad += down.astype(jnp.float32)
            lo, hi = bounds[f]
            gate_wide = gate_act[:, lo:hi].astype(jnp.float32)
            up_wide = up_act[:, lo:hi].astype(jnp.float32)
            sigmoid_gate = jax.nn.sigmoid(gate_wide)
            up_parts.append((hidden_grad * gate_wide * sigmoid_gate).astype(jnp.bfloat16))
            gate_parts.append(
                (
                    hidden_grad * up_wide * sigmoid_gate * (1.0 + gate_wide * (1.0 - sigmoid_gate))
                ).astype(jnp.bfloat16)
            )

        out_slots = jnp.concatenate(outs, axis=1)

        def half_of(step):
            first = (x + step) % n_local * per_half
            starts = [(far - first - q) % n_far * columns for q in range(per_half)]
            return jnp.concatenate(
                [lax.dynamic_slice_in_dim(out_slots, s, columns, axis=1) for s in starts], axis=1
            )

        sides = [local_shift(half_of(step), step) for step in range(1, n_local)]
        output = half_of(0).astype(jnp.float32)
        for side in sides:
            output = output + side.astype(jnp.float32)
        output = output.astype(jnp.bfloat16).reshape(tokens, per_half, QUAD, width)
        return (
            picked(output, slot_of(near), 2).reshape(tokens, half),
            jnp.concatenate(gate_parts, axis=1),
            jnp.concatenate(up_parts, axis=1),
            down_grad,
        )

    specs = (P("hst", "local"), P("hst", "local"), P("hst", "local"), P("local", "hst"))
    return jax.shard_map(
        on_device, mesh=mesh, in_specs=specs, out_specs=specs, check_vma=False
    )
```

```python
import jax
import jax.numpy as jnp
from jax import lax
from jax.sharding import PartitionSpec as P

QUAD = 4
ORDER = (0, 2, 1, 3)
KEEP_COLS = (((1,), (1,)), ((), ()))
SUM_ROWS = (((0,), (0,)), ((), ()))


def after(value, *others):
    return lax.optimization_barrier((value,) + others)[0] if others else value


def slot_of(near):
    return [((near ^ block) & 1) << 1 | (near ^ block) >> 1 for block in range(QUAD)]


def picked(view, places, axis):
    return jnp.concatenate(
        [lax.dynamic_slice_in_dim(view, place, 1, axis=axis) for place in places], axis=axis
    )


def solution(mesh):
    n_hst, n_local = mesh.shape["hst"], mesh.shape["local"]
    n_far = n_hst // QUAD
    last_hop = n_far - 1

    def swap(value, bit):
        return lax.ppermute(value, "hst", [(h, h ^ bit) for h in range(n_hst)])

    def shift(value, step):
        pairs = [(h, (h + step * QUAD) % n_hst) for h in range(n_hst)]
        return lax.ppermute(value, "hst", pairs)

    def far_permute(value, pairs):
        pairs = [(s * QUAD + q, t * QUAD + q) for s, t in pairs for q in range(QUAD)]
        return lax.ppermute(value, "hst", pairs)

    def both_ways(up, down, sources):
        return (
            far_permute(up, [(z, z + 1) for z in sources]),
            far_permute(down, [(n_far - 1 - z, n_far - 2 - z) for z in sources]),
        )

    def local_shift(value, step):
        return lax.ppermute(value, "local", [(i, (i + step) % n_local) for i in range(n_local)])

    def on_device(gate_act, up_act, cotangent, down_weight):
        h = lax.axis_index("hst")
        x = lax.axis_index("local")
        far, near = h // QUAD, h % QUAD
        tokens, half = cotangent.shape
        width = down_weight.shape[1]
        columns = QUAD * width
        hidden_units = gate_act.shape[1]
        per_half = half // columns
        middle = 128 * ((hidden_units // 128 + 1) // 2)
        bounds = [(0, middle), (middle, hidden_units)]

        fence = []

        def move(send, value, *args):
            return send(after(value, *fence), *args)

        gate_all, up_all = gate_act.astype(jnp.float32), up_act.astype(jnp.float32)
        hidden = (gate_all * jax.nn.sigmoid(gate_all) * up_all).astype(jnp.bfloat16)
        lower = far < n_far // 2

        above, below, travel = {}, {}, {}

        def gather_hop(j):
            up, down = (below[j - 1], above[j - 1]) if j > 1 else (hidden, hidden)
            if j == last_hop:
                one = after(jnp.where(lower, down, up), *fence)
                ends = [(n_far - 2, n_far - 1), (1, 0)]
                below[j] = above[j] = far_permute(one, ends)
                return [below[j]]
            up, down = after(up, *fence), after(down, *fence)
            below[j], above[j] = both_ways(up, down, range(j - 1, n_far - 1))
            return [below[j], above[j]]

        def reduce_hop(f, j):
            d = n_far - j
            up_term, down_term = terms[f][d], terms[f][n_far - d]
            if j == 1:
                one = after(jnp.where(lower, up_term, down_term), *fence)
                one = far_permute(one, [(0, 1), (n_far - 1, n_far - 2)])
                none = jnp.zeros_like(one)
                travel[f] = jnp.where(lower, one, none), jnp.where(lower, none, one)
                return [one]
            up, down = travel[f]
            up_term = (up_term.astype(jnp.float32) + up.astype(jnp.float32)).astype(jnp.bfloat16)
            down_term = down_term.astype(jnp.float32) + down.astype(jnp.float32)
            down_term = down_term.astype(jnp.bfloat16)
            up_term, down_term = after(up_term, *fence), after(down_term, *fence)
            travel[f] = both_ways(up_term, down_term, range(0, j))
            return list(travel[f])

        def weight_columns(f, other):
            lo, hi = bounds[f]
            pair = jnp.concatenate([down_weight[lo:hi], other], axis=1)
            far_pairs[f] = move(swap, pair, 1)
            return jnp.concatenate([pair, far_pairs[f]], axis=1)

        def reduce_terms(f):
            dots = lax.dot_general(
                cot_rows, weights[f], KEEP_COLS, preferred_element_type=jnp.float32
            ).astype(jnp.bfloat16)
            return [dots[e * tokens : (e + 1) * tokens] for e in range(n_far)]

        weights, far_pairs, terms = {}, {}, {}

        parts = [cotangent] + [local_shift(cotangent, n_local - s) for s in range(1, n_local)]
        weight_side = swap(after(down_weight[:middle], hidden), 2)
        waits = gather_hop(1)
        cot_slots = jnp.concatenate(parts, axis=1).reshape(tokens, n_far, QUAD, width)
        cot_slots = picked(cot_slots, [near ^ k for k in ORDER], 2).reshape(tokens, n_far, columns)

        block = tokens // n_local

        def cot_for(step, first_row, count):
            place = (far + step) % n_far
            start = (place // per_half - x) % n_local * per_half + place % per_half
            found = lax.dynamic_slice(cot_slots, (first_row, start, 0), (count, 1, columns))
            return found.reshape(count, columns)

        came = []
        for e in range(1, n_far):
            sent = cot_for(n_far - e, x * block, block)
            came.append(shift(after(sent, *came[: max(0, e - 2)]), n_far - e))
        second_weight = lax.optimization_barrier(down_weight[middle:])
        fence = waits + came + [weight_side, second_weight]

        def whole_rows():
            mine = jnp.concatenate(came, axis=0)
            sides = [mine] + [move(local_shift, mine, n_local - i) for i in range(1, n_local)]
            blocks = []
            for i in range(n_local):
                picked_block = sides[0]
                for turn in range(1, n_local):
                    here = (i - x) % n_local == turn
                    picked_block = jnp.where(here, sides[turn], picked_block)
                blocks.append(picked_block.reshape(n_far - 1, block, columns))
            others = jnp.concatenate(blocks, axis=1).reshape((n_far - 1) * tokens, columns)
            return jnp.concatenate([cot_for(0, 0, tokens), others], axis=0)

        for j in range(2, n_far):
            waits = gather_hop(j)
            if j == 2:
                cot_rows = whole_rows()
                weights[0] = weight_columns(0, weight_side)
                weight_side = move(swap, second_weight, 2)
                terms[0] = reduce_terms(0)
                waits.append(weight_side)
            if j == 3:
                weights[1] = weight_columns(1, weight_side)
                terms[1] = reduce_terms(1)
                fence = fence + [far_pairs[1]]
            waits += reduce_hop(0, j - 1)
            if j > 2:
                waits += reduce_hop(1, j - 2)
            fence = waits

        gather_fence, fence = fence, []
        waits = reduce_hop(0, last_hop)
        fence = gather_fence
        waits += reduce_hop(1, last_hop - 1)
        slots = [after(hidden, *fence)]
        for e in range(1, n_far):
            above_e, below_e = after(above[e], *fence), after(below[n_far - e], *fence)
            slots.append(jnp.where(far + e < n_far, above_e, below_e))
        rows = jnp.concatenate(slots, axis=0)

        def grad_terms(lo, hi):
            part = cot_rows[:, lo * width : hi * width]
            return lax.dot_general(rows, part, SUM_ROWS, preferred_element_type=jnp.float32)

        theirs = swap(after(grad_terms(2, 4).astype(jnp.bfloat16), *travel[0]), 1)
        give = grad_terms(1, 2) + theirs[:, width:].astype(jnp.float32)
        give = give.astype(jnp.bfloat16)
        other_grad = swap(give, 2)
        rows = after(rows, give)
        down_grad = grad_terms(0, 1) + after(theirs, give)[:, :width].astype(jnp.float32)
        down_grad = down_grad + other_grad.astype(jnp.float32)
        out_sum = 0.0
        for f, (lo, hi) in enumerate(bounds):
            out_sum += jnp.dot(rows[:, lo:hi], weights[f], preferred_element_type=jnp.float32)
            if f == 0:
                for part in travel:
                    travel[part] = tuple(after(value, out_sum) for value in travel[part])
        out_terms = after(out_sum.astype(jnp.bfloat16), *waits)

        fence = waits + [give, out_terms]
        waits = reduce_hop(1, last_hop)
        outs = [out_terms[:tokens]]
        for e in range(1, n_far):
            term = out_terms[e * tokens : (e + 1) * tokens]
            outs.append(shift(after(term, *outs[1 : max(1, e - 1)]), e))
        up_parts, gate_parts = [], []
        for f in range(2):
            up, down = travel[f]
            hidden_grad = terms[f][0].astype(jnp.float32) + up.astype(jnp.float32)
            hidden_grad += down.astype(jnp.float32)
            lo, hi = bounds[f]
            gate_wide = gate_act[:, lo:hi].astype(jnp.float32)
            up_wide = up_act[:, lo:hi].astype(jnp.float32)
            sigmoid_gate = jax.nn.sigmoid(gate_wide)
            up_parts.append((hidden_grad * gate_wide * sigmoid_gate).astype(jnp.bfloat16))
            gate_parts.append(
                (
                    hidden_grad * up_wide * sigmoid_gate * (1.0 + gate_wide * (1.0 - sigmoid_gate))
                ).astype(jnp.bfloat16)
            )

        out_slots = jnp.concatenate(outs, axis=1)

        def half_of(step):
            first = (x + step) % n_local * per_half
            starts = [(far - first - q) % n_far * columns for q in range(per_half)]
            return jnp.concatenate(
                [lax.dynamic_slice_in_dim(out_slots, s, columns, axis=1) for s in starts], axis=1
            )

        sides = [local_shift(half_of(step), step) for step in range(1, n_local)]
        output = half_of(0).astype(jnp.float32)
        for side in sides:
            output = output + after(side, down_grad).astype(jnp.float32)
        output = output.astype(jnp.bfloat16).reshape(tokens, per_half, QUAD, width)
        return (
            picked(output, slot_of(near), 2).reshape(tokens, half),
            jnp.concatenate(gate_parts, axis=1),
            jnp.concatenate(up_parts, axis=1),
            down_grad,
        )

    specs = (P("hst", "local"), P("hst", "local"), P("hst", "local"), P("local", "hst"))
    return jax.shard_map(
        on_device, mesh=mesh, in_specs=specs, out_specs=specs, check_vma=False
    )
```

```python
import jax
import jax.numpy as jnp
from jax import lax
from jax.sharding import PartitionSpec as P

QUAD = 4
ORDER = (0, 2, 1, 3)
KEEP_COLS = (((1,), (1,)), ((), ()))
SUM_ROWS = (((0,), (0,)), ((), ()))


def after(value, *others):
    return lax.optimization_barrier((value,) + others)[0] if others else value


def slot_of(near):
    return [((near ^ block) & 1) << 1 | (near ^ block) >> 1 for block in range(QUAD)]


def picked(view, places, axis):
    return jnp.concatenate(
        [lax.dynamic_slice_in_dim(view, place, 1, axis=axis) for place in places], axis=axis
    )


def solution(mesh):
    n_hst, n_local = mesh.shape["hst"], mesh.shape["local"]
    n_far = n_hst // QUAD
    last_hop = n_far - 1

    def swap(value, bit):
        return lax.ppermute(value, "hst", [(h, h ^ bit) for h in range(n_hst)])

    def shift(value, step):
        pairs = [(h, (h + step * QUAD) % n_hst) for h in range(n_hst)]
        return lax.ppermute(value, "hst", pairs)

    def far_permute(value, pairs):
        pairs = [(s * QUAD + q, t * QUAD + q) for s, t in pairs for q in range(QUAD)]
        return lax.ppermute(value, "hst", pairs)

    def both_ways(up, down, sources):
        return (
            far_permute(up, [(z, z + 1) for z in sources]),
            far_permute(down, [(n_far - 1 - z, n_far - 2 - z) for z in sources]),
        )

    def local_shift(value, step):
        return lax.ppermute(value, "local", [(i, (i + step) % n_local) for i in range(n_local)])

    def on_device(gate_act, up_act, cotangent, down_weight):
        h = lax.axis_index("hst")
        x = lax.axis_index("local")
        far, near = h // QUAD, h % QUAD
        tokens, half = cotangent.shape
        width = down_weight.shape[1]
        columns = QUAD * width
        hidden_units = gate_act.shape[1]
        per_half = half // columns
        middle = 128 * (hidden_units // 128 * 15 // 32)
        bounds = [(0, middle), (middle, hidden_units)]

        fence = []

        def move(send, value, *args):
            return send(after(value, *fence), *args)

        gate_all, up_all = gate_act.astype(jnp.float32), up_act.astype(jnp.float32)
        hidden = (gate_all * jax.nn.sigmoid(gate_all) * up_all).astype(jnp.bfloat16)
        lower = far < n_far // 2

        above, below, travel = {}, {}, {}

        def gather_hop(j):
            up, down = (below[j - 1], above[j - 1]) if j > 1 else (hidden, hidden)
            if j == last_hop:
                one = after(jnp.where(lower, down, up), *fence)
                ends = [(n_far - 2, n_far - 1), (1, 0)]
                below[j] = above[j] = far_permute(one, ends)
                return [below[j]]
            up, down = after(up, *fence), after(down, *fence)
            below[j], above[j] = both_ways(up, down, range(j - 1, n_far - 1))
            return [below[j], above[j]]

        def reduce_hop(f, j):
            d = n_far - j
            up_term, down_term = terms[f][d], terms[f][n_far - d]
            if j == 1:
                one = after(jnp.where(lower, up_term, down_term), *fence)
                one = far_permute(one, [(0, 1), (n_far - 1, n_far - 2)])
                none = jnp.zeros_like(one)
                travel[f] = jnp.where(lower, one, none), jnp.where(lower, none, one)
                return [one]
            up, down = travel[f]
            up_term = (up_term.astype(jnp.float32) + up.astype(jnp.float32)).astype(jnp.bfloat16)
            down_term = down_term.astype(jnp.float32) + down.astype(jnp.float32)
            down_term = down_term.astype(jnp.bfloat16)
            up_term, down_term = after(up_term, *fence), after(down_term, *fence)
            travel[f] = both_ways(up_term, down_term, range(0, j))
            return list(travel[f])

        def weight_columns(f, other):
            lo, hi = bounds[f]
            pair = jnp.concatenate([down_weight[lo:hi], other], axis=1)
            far_pairs[f] = move(swap, pair, 1)
            return jnp.concatenate([pair, far_pairs[f]], axis=1)

        def reduce_terms(f):
            dots = lax.dot_general(
                cot_rows, weights[f], KEEP_COLS, preferred_element_type=jnp.float32
            ).astype(jnp.bfloat16)
            return [dots[e * tokens : (e + 1) * tokens] for e in range(n_far)]

        weights, far_pairs, terms = {}, {}, {}

        parts = [cotangent] + [local_shift(cotangent, n_local - s) for s in range(1, n_local)]
        weight_side = swap(after(down_weight[:middle], hidden), 2)
        waits = gather_hop(1)
        cot_slots = jnp.concatenate(parts, axis=1).reshape(tokens, n_far, QUAD, width)
        cot_slots = picked(cot_slots, [near ^ k for k in ORDER], 2).reshape(tokens, n_far, columns)

        block = tokens // n_local

        def cot_for(step, first_row, count):
            place = (far + step) % n_far
            start = (place // per_half - x) % n_local * per_half + place % per_half
            found = lax.dynamic_slice(cot_slots, (first_row, start, 0), (count, 1, columns))
            return found.reshape(count, columns)

        came = []
        for e in range(1, n_far):
            sent = cot_for(n_far - e, x * block, block)
            came.append(shift(after(sent, *came[: max(0, e - 2)]), n_far - e))
        second_weight = lax.optimization_barrier(down_weight[middle:])
        fence = waits + came + [weight_side, second_weight]

        def whole_rows():
            mine = jnp.concatenate(came, axis=0)
            sides = [mine] + [move(local_shift, mine, n_local - i) for i in range(1, n_local)]
            blocks = []
            for i in range(n_local):
                picked_block = sides[0]
                for turn in range(1, n_local):
                    here = (i - x) % n_local == turn
                    picked_block = jnp.where(here, sides[turn], picked_block)
                blocks.append(picked_block.reshape(n_far - 1, block, columns))
            others = jnp.concatenate(blocks, axis=1).reshape((n_far - 1) * tokens, columns)
            return jnp.concatenate([cot_for(0, 0, tokens), others], axis=0)

        for j in range(2, n_far):
            waits = gather_hop(j)
            if j == 2:
                cot_rows = whole_rows()
                weights[0] = weight_columns(0, weight_side)
                weight_side = move(swap, second_weight, 2)
                terms[0] = reduce_terms(0)
                waits.append(weight_side)
            if j == 3:
                weights[1] = weight_columns(1, weight_side)
                terms[1] = reduce_terms(1)
                fence = fence + [far_pairs[1]]
            waits += reduce_hop(0, j - 1)
            if j > 2:
                waits += reduce_hop(1, j - 2)
            fence = waits

        gather_fence, fence = fence, []
        waits = reduce_hop(0, last_hop)
        fence = gather_fence
        waits += reduce_hop(1, last_hop - 1)
        slots = [after(hidden, *fence)]
        for e in range(1, n_far):
            above_e, below_e = after(above[e], *fence), after(below[n_far - e], *fence)
            slots.append(jnp.where(far + e < n_far, above_e, below_e))
        rows = jnp.concatenate(slots, axis=0)

        def grad_terms(lo, hi):
            part = cot_rows[:, lo * width : hi * width]
            return lax.dot_general(rows, part, SUM_ROWS, preferred_element_type=jnp.float32)

        theirs = swap(after(grad_terms(2, 4).astype(jnp.bfloat16), *travel[0]), 1)
        give = grad_terms(1, 2) + theirs[:, width:].astype(jnp.float32)
        give = give.astype(jnp.bfloat16)
        other_grad = swap(give, 2)
        rows = after(rows, give)
        down_grad = grad_terms(0, 1) + after(theirs, give)[:, :width].astype(jnp.float32)
        down_grad = down_grad + other_grad.astype(jnp.float32)
        out_sum = 0.0
        for f, (lo, hi) in enumerate(bounds):
            out_sum += jnp.dot(rows[:, lo:hi], weights[f], preferred_element_type=jnp.float32)
            if f == 0:
                for part in travel:
                    travel[part] = tuple(after(value, out_sum) for value in travel[part])
        out_terms = after(out_sum.astype(jnp.bfloat16), *waits)

        fence = waits + [give, out_terms]
        waits = reduce_hop(1, last_hop)
        outs = [out_terms[:tokens]]
        for e in range(1, n_far):
            term = out_terms[e * tokens : (e + 1) * tokens]
            outs.append(shift(after(term, *outs[1 : max(1, e - 1)]), e))
        up_parts, gate_parts = [], []
        for f in range(2):
            up, down = travel[f]
            hidden_grad = terms[f][0].astype(jnp.float32) + up.astype(jnp.float32)
            hidden_grad += down.astype(jnp.float32)
            lo, hi = bounds[f]
            gate_wide = gate_act[:, lo:hi].astype(jnp.float32)
            up_wide = up_act[:, lo:hi].astype(jnp.float32)
            sigmoid_gate = jax.nn.sigmoid(gate_wide)
            up_parts.append((hidden_grad * gate_wide * sigmoid_gate).astype(jnp.bfloat16))
            gate_parts.append(
                (
                    hidden_grad * up_wide * sigmoid_gate * (1.0 + gate_wide * (1.0 - sigmoid_gate))
                ).astype(jnp.bfloat16)
            )

        out_slots = jnp.concatenate(outs, axis=1)

        def half_of(step):
            first = (x + step) % n_local * per_half
            starts = [(far - first - q) % n_far * columns for q in range(per_half)]
            return jnp.concatenate(
                [lax.dynamic_slice_in_dim(out_slots, s, columns, axis=1) for s in starts], axis=1
            )

        sides = [local_shift(half_of(step), step) for step in range(1, n_local)]
        output = half_of(0).astype(jnp.float32)
        for side in sides:
            output = output + after(side, down_grad).astype(jnp.float32)
        output = output.astype(jnp.bfloat16).reshape(tokens, per_half, QUAD, width)
        return (
            picked(output, slot_of(near), 2).reshape(tokens, half),
            jnp.concatenate(gate_parts, axis=1),
            jnp.concatenate(up_parts, axis=1),
            down_grad,
        )

    specs = (P("hst", "local"), P("hst", "local"), P("hst", "local"), P("local", "hst"))
    return jax.shard_map(
        on_device, mesh=mesh, in_specs=specs, out_specs=specs, check_vma=False
    )
```
